32 devices in a mesh: param: 8 (over y, x, core), proj: 4 (over z).
Axes of the slice: x: 2, y: 2, z: 4, core: 2. Of those that a mesh axis runs over, the one named last changes fastest.
Arguments:
- query_grads: float32 [256, 65536], P(None, 'param'), may hold values from -45 to 45, as said below
- stored: float32 [8192, 4096], P('param', 'proj'), may hold values from -6 to 6
- proj_seed: int32 [2], replicated, may hold values from 0 to 32748
- offsets: int32 [8], P('param'), may hold values from 0 to 32748
Outputs:
- similarity: float32 [256, 8192], P('proj', 'param')
The draws below stay inside these ranges and needn't reach their ends.
Inputs may be any that keep to these rules, and one draw needn't show every extreme that they name: `query_grads`: query gradients have row and coordinate scales that differ.
All inputs are finite; a program needn't handle non-finite values.
Results may differ from the reference program's by a relative error of at most 0.0003.
Values sent between devices are 32-bit elements; how exact they have to be, the bound alone decides.
A program may use at most 128 MiB of HBM per device.

```python
import math
import jax
import jax.numpy as jnp
from jax import lax

QUERIES = 256
PARAMS = 65536
PWIDTH = 4096
STORE = 8192
N_PARAM = 8
N_PROJ = 4


def draw_query_grads(key, part):
    keys = jax.random.split(key, 3)
    row_scale = jnp.exp(jax.random.uniform(keys[0], (QUERIES, 1), jnp.float32) * math.log(10.0))
    column_scale = jnp.exp(jax.random.uniform(keys[1], (1, PARAMS), jnp.float32) * math.log(10.0))
    values = jax.random.truncated_normal(keys[2], -4.0, 4.0, (QUERIES, PARAMS), jnp.float32)
    return values * row_scale * column_scale / 10.0


def set_ends(array, key, least, high):
    extent = array.shape
    spot = [jax.random.randint(jax.random.fold_in(key, axis), (), 0, extent[axis]) for axis in range(len(extent))]
    array = array.at[tuple(spot)].set(least)
    longest = extent.index(max(extent))
    spot[longest] = (spot[longest] + 1) % extent[longest]
    return array.at[tuple(spot)].set(high)


def block_levels(stream_key, dims, shards, low, largest):
    def one(dim, shards_of):
        heights = jax.random.uniform(jax.random.fold_in(jax.random.fold_in(stream_key, 6), dim), (shards_of,), jnp.float32, low / len(shards), largest / len(shards))
        return jnp.repeat(jnp.exp(heights), dims[dim] // shards_of).reshape((-1,) + (1,) * (len(dims) - dim - 1))

    loudness = one(*shards[0])
    for cut in shards[1:]:
        loudness = loudness * one(*cut)
    return loudness


def gaussian(rng, shape, width, most, shards=(), kind=jnp.bfloat16):
    array = jax.random.normal(rng, shape, jnp.float32) * width
    if len(shards) > 0:
        array = block_levels(rng, shape, shards, -0.22, 0.18) * array
    return jnp.clip(array, min=-most, max=most).astype(kind)


def setup_inputs(seed: int = 0) -> dict:
    key_list = jax.random.split(jax.random.key(seed), 5)
    return {
        "query_grads": draw_query_grads(jax.random.fold_in(key_list[4], 71), 0),
        "stored": gaussian(key_list[1], (STORE, PWIDTH), 1.0, 6.0, ((0, 8), (1, 4)), jnp.float32),
        "proj_seed": jax.random.randint(key_list[2], (2,), 0, 32749).astype(jnp.int32),
        "offsets": set_ends(jax.random.randint(key_list[3], (N_PARAM,), 0, 32749), jax.random.fold_in(key_list[3], 1), 0, 32748).astype(jnp.int32),
    }


modulus = 32749
epsilon = 1e-06

def proj_tile(offset, proj_seed, column_start, coords_count, width_count, param_total, width_total):
    coord_ids = jnp.arange(coords_count, dtype=jnp.int32)[:, None] + offset
    column_ids = column_start + jnp.arange(width_count, dtype=jnp.int32)[None, :]
    coord_hash = (coord_ids * 1103 + proj_seed[0]) % modulus
    column_hash = (column_ids * 2111 + proj_seed[1]) % modulus
    mixed = (coord_hash * column_hash + coord_hash + 3 * column_hash + 17) % modulus
    mixed = (mixed * mixed + coord_hash) % modulus
    uniform_val = (mixed.astype(jnp.float32) + 0.5) * (2.0 / modulus) - 1.0
    column_gain = jnp.sqrt(1.0 + 2.0 * column_ids.astype(jnp.float32) / width_total)
    return uniform_val * column_gain * math.sqrt(3.0 / param_total)

def reference(query_grads, stored, proj_seed, offsets):
    queries, param_total = query_grads.shape
    blocks = offsets.shape[0]
    coords_dev = param_total // blocks
    width_total = stored.shape[1]
    width_dev = width_total // N_PROJ

    def column_block(column_index):
        column_start = column_index * width_dev

        def add_block(accum, block_id):
            piece = proj_tile(offsets[block_id], proj_seed, column_start, coords_dev, width_dev, param_total, width_total)
            grads = lax.dynamic_slice_in_dim(query_grads, block_id * coords_dev, coords_dev, 1)
            return (accum + jnp.dot(grads, piece, precision=lax.Precision.HIGHEST, preferred_element_type=jnp.float32), None)
        accum, _ = lax.scan(add_block, jnp.zeros((queries, width_dev), jnp.float32), jnp.arange(blocks, dtype=jnp.int32))
        return accum
    stacked = lax.map(column_block, jnp.arange(N_PROJ, dtype=jnp.int32))
    projected = jnp.transpose(stacked, (1, 0, 2)).reshape(queries, width_total)
    inverse = lax.rsqrt(lax.optimization_barrier(jnp.mean(projected * projected, axis=1, keepdims=True)) + epsilon)
    raw_scores = lax.dot_general(projected, stored, (((1,), (1,)), ((), ())), precision=lax.Precision.HIGHEST, preferred_element_type=jnp.float32)
    return jnp.tanh(raw_scores * inverse / math.sqrt(width_total))
```

```python
import functools
import math

import jax
import jax.numpy as jnp
import numpy as np
from jax import lax
from jax.experimental import pallas as pl
from jax.experimental.pallas import tpu as pltpu
from jax.sharding import PartitionSpec as P

modulus = 32749
middle = modulus // 2
epsilon = 1e-06
bits = 8
block = 1 << bits
pairs = [(p, q) for p in range(bits) for q in range(p + 1, bits)]
pair_rows = 64
vary_rows = 32
slab_blocks = 4


def centred(value):
    value = value % modulus
    return jnp.where(value > middle, value - modulus, value)


def two_pieces(value):
    low = ((value + 64) & 127) - 64
    return (value - low).astype(jnp.bfloat16), low.astype(jnp.bfloat16)


def bit_features():
    digits = (np.arange(block)[:, None] >> np.arange(bits)[None, :]) & 1
    cross = np.stack([digits[:, p] * digits[:, q] for p, q in pairs], axis=1)
    vary = np.concatenate([digits, np.ones((block, 1), digits.dtype)], axis=1)
    out = np.zeros((block, 128), np.float32)
    out[:, : len(pairs)] = cross
    out[:, len(pairs) : 2 * len(pairs)] = cross
    out[:, pair_rows : pair_rows + bits + 1] = vary
    out[:, pair_rows + bits + 1 : pair_rows + 2 * (bits + 1)] = vary
    return jnp.asarray(out, jnp.bfloat16)


def coefficients(offset, proj_seed, column_start, coords, width):
    column = column_start + jnp.arange(width, dtype=jnp.int32)[None, :]
    start = (offset * 1103 + proj_seed[0]) % modulus
    factor = ((column * 2111 + proj_seed[1]) % modulus) + 1
    slope = (factor * 1103) % modulus
    level = ((start + 3) * factor + 14) % modulus
    square = (slope * slope) % modulus
    linear = ((slope * level) % modulus * 2 + 1103) % modulus
    constant = (level * level + start) % modulus
    base = ((jnp.arange(coords // block, dtype=jnp.int32) * block) % modulus)[:, None]
    linear_at = (linear + (square * base) % modulus * 2) % modulus
    constant_at = (((square * base) % modulus + linear) % modulus * base + constant) % modulus
    cross = centred(
        jnp.concatenate([(square * (2 ** (p + q + 1))) % modulus for p, q in pairs], axis=0)
    )
    vary = [centred((square * 4**p) % modulus + linear_at * 2**p) for p in range(bits)]
    vary.append(centred(constant_at - middle))
    vary = jnp.stack(vary, axis=1)
    cross_high, cross_low = two_pieces(cross)
    vary_high, vary_low = two_pieces(vary)
    cross = jnp.concatenate([cross_high, cross_low], axis=0)
    cross = jnp.pad(cross, ((0, pair_rows - cross.shape[0]), (0, 0)))
    vary = jnp.concatenate([vary_high, vary_low], axis=1)
    vary = jnp.pad(vary, ((0, 0), (0, vary_rows - vary.shape[1]), (0, 0)))
    return cross, vary


def project_kernel(chunk, feat_ref, cross_ref, vary_ref, gain_ref, grads_ref, out_ref,
                   stage, high_q, low_q, high_a, low_a, high_b, low_b, total, sems):
    queries, coords = high_q.shape
    width = out_ref.shape[1]
    slab = block * slab_blocks
    slabs = coords // slab

    def fetch(s):
        return pltpu.make_async_copy(
            grads_ref.at[:, pl.ds(pl.multiple_of(s * slab, slab), slab)], stage.at[s], sems.at[s]
        )

    def make(s, column, high, low):
        cross = cross_ref[:, pl.ds(column, chunk)]
        blank = jnp.zeros((128 - pair_rows - vary_rows, chunk), jnp.bfloat16)
        for part in range(slab_blocks):
            vary = vary_ref[s * slab_blocks + part, :, pl.ds(column, chunk)]
            coef = jnp.concatenate([cross, vary, blank], axis=0)
            x = jnp.dot(feat_ref[...], coef, preferred_element_type=jnp.float32)
            x = x * (1.0 / modulus)
            x = x - jnp.round(x)
            top = x.astype(jnp.bfloat16)
            high[pl.ds(part * block, block), :] = top
            low[pl.ds(part * block, block), :] = (x - top.astype(jnp.float32)).astype(jnp.bfloat16)

    def use(s, high, low):
        at = pl.ds(pl.multiple_of(s * slab, slab), slab)
        qh = high_q[:, at]
        ql = low_q[:, at]
        wh = high[...]
        wl = low[...]
        total[...] += (
            jnp.dot(qh, wh, preferred_element_type=jnp.float32)
            + jnp.dot(ql, wh, preferred_element_type=jnp.float32)
            + jnp.dot(qh, wl, preferred_element_type=jnp.float32)
        )

    for s in range(slabs):
        fetch(s).start()

    @pl.loop(0, slabs)
    def _(s):
        fetch(s).wait()
        at = pl.ds(pl.multiple_of(s * slab, slab), slab)
        q = stage[s]
        top = q.astype(jnp.bfloat16)
        high_q[:, at] = top
        low_q[:, at] = (q - top.astype(jnp.float32)).astype(jnp.bfloat16)

    @pl.loop(0, width // chunk)
    def _(n):
        column = pl.multiple_of(n * chunk, chunk)
        total[...] = jnp.zeros_like(total)
        make(0, column, high_a, low_a)

        @pl.loop(0, slabs // 2)
        def _(pair):
            s = pair * 2
            make(s + 1, column, high_b, low_b)
            use(s, high_a, low_a)
            make(lax.rem(s + 2, slabs), column, high_a, low_a)
            use(s + 1, high_b, low_b)

        out_ref[:, pl.ds(column, chunk)] = total[...] * gain_ref[:, pl.ds(column, chunk)]


def project(query_grads, cross, vary, gain):
    queries, coords = query_grads.shape
    width = gain.shape[1]
    chunk = 256
    slab = block * slab_blocks
    vmem = pl.BlockSpec(memory_space=pltpu.VMEM)
    half = pltpu.VMEM((slab, chunk), jnp.bfloat16)
    return pl.pallas_call(
        functools.partial(project_kernel, chunk),
        out_shape=jax.ShapeDtypeStruct((queries, width), jnp.float32),
        in_specs=[vmem] * 4 + [pl.BlockSpec(memory_space=pl.ANY)],
        out_specs=vmem,
        scratch_shapes=[
            pltpu.VMEM((coords // slab, queries, slab), jnp.float32),
            pltpu.VMEM((queries, coords), jnp.bfloat16),
            pltpu.VMEM((queries, coords), jnp.bfloat16),
            half, half, half, half,
            pltpu.VMEM((queries, chunk), jnp.float32),
            pltpu.SemaphoreType.DMA((coords // slab,)),
        ],
        compiler_params=pltpu.CompilerParams(vmem_limit_bytes=48 * 1024 * 1024),
        name="project",
    )(bit_features(), cross, vary, gain, query_grads)


def on_device(query_grads, stored, proj_seed, offsets):
    n_param = lax.axis_size("param")
    n_proj = lax.axis_size("proj")
    queries, coords = query_grads.shape
    store_rows, width = stored.shape
    param_total = coords * n_param
    width_total = width * n_proj
    column_start = lax.axis_index("proj") * width
    cross, vary = coefficients(offsets[0], proj_seed, column_start, coords, width)
    column = (column_start + jnp.arange(width, dtype=jnp.int32)[None, :]).astype(jnp.float32)
    gain = jnp.sqrt(1.0 + 2.0 * column / width_total) * (2.0 * math.sqrt(3.0 / param_total))
    local = project(query_grads, cross, vary, gain)
    projected = lax.psum(local, "param")
    raw = lax.dot_general(
        projected, stored, (((1,), (1,)), ((), ())),
        precision=lax.Precision.HIGH, preferred_element_type=jnp.float32,
    )
    squares = jnp.sum(projected * projected, axis=1, keepdims=True)
    squares = lax.psum_scatter(squares, "proj", scatter_dimension=0, tiled=True)
    inverse = lax.rsqrt(squares / width_total + epsilon)
    summed = lax.psum_scatter(raw, "proj", scatter_dimension=0, tiled=True)
    return jnp.tanh(summed * (inverse * (1.0 / math.sqrt(width_total))))


def solution(mesh):
    placed = (P(None, "param"), P("param", "proj"), P(), P("param"))
    return jax.shard_map(
        on_device, mesh=mesh, in_specs=placed, out_specs=P("proj", "param"), check_vma=False
    )
```

```python
import functools
import math

import jax
import jax.numpy as jnp
import numpy as np
from jax import lax
from jax.experimental import pallas as pl
from jax.experimental.pallas import tpu as pltpu
from jax.sharding import PartitionSpec as P

modulus = 32749
middle = modulus // 2
epsilon = 1e-06
bits = 8
block = 1 << bits
pairs = [(p, q) for p in range(bits) for q in range(p + 1, bits)]
slab_blocks = 4
slab = block * slab_blocks
chunk = 256
pieces = 2
MESH = pl.DeviceIdType.MESH


def bit_features():
    digits = (np.arange(block)[:, None] >> np.arange(bits)[None, :]) & 1
    cross = np.stack([digits[:, p] * digits[:, q] for p, q in pairs], axis=1)
    vary = np.concatenate([digits, np.ones((block, 1), digits.dtype)], axis=1)
    out = np.zeros((block, 128), np.float32)
    for at in (0, 32):
        out[:, at : at + len(pairs)] = cross
    for at in (64, 80):
        out[:, at : at + bits + 1] = vary
    return jnp.asarray(out, jnp.bfloat16)


def pair_weights():
    out = np.zeros((32, 128), np.int32)
    for row, (p, q) in enumerate(pairs):
        out[row] = 2 ** (p + q + 1)
    return jnp.asarray(out)


def reduced(value):
    times = jnp.round(value.astype(jnp.float32) * (1.0 / modulus)).astype(jnp.int32)
    return value - times * modulus


def reduced_float(value):
    return value - jnp.round(value * (1.0 / modulus)) * modulus


def two_pieces(value):
    high = jnp.round(value * (1.0 / 128)) * 128.0
    return high.astype(jnp.bfloat16), (value - high).astype(jnp.bfloat16)


def split(value):
    high = value.astype(jnp.bfloat16)
    return high, (value - high.astype(jnp.float32)).astype(jnp.bfloat16)


def mix(a, b):
    return jnp.dot(a, b, preferred_element_type=jnp.float32)


def mix_rows(a, b):
    return lax.dot_general(a, b, (((1,), (1,)), ((), ())), preferred_element_type=jnp.float32)


def kernel(n_param, n_proj, offset_ref, seed_ref, feat_ref, weight_ref, grads_ref, stored_ref, out_ref,
           stage, store, high_q, low_q, cross, vary, high_a, low_a, high_b, low_b, total,
           part, pair_in, ring_in, proj, raw, square_out, square_in, column_sum, line_in,
           grad_sem, store_sem, pair_sem, ring_sem, gather_sem, back_sem, square_sem, line_sem):
    queries, coords = high_q.shape
    store_rows, width = store.shape
    slabs = coords // slab
    chunks = width // chunk
    chips = n_param // 2
    half = queries // 2
    own = half // chips
    share = queries // n_proj
    piece = share // pieces
    me = lax.axis_index("param")
    here = lax.axis_index("proj")
    core = lax.rem(me, 2)
    chip = lax.div(me, 2)
    sibling = me + 1 - 2 * core
    width_total = width * n_proj
    scale = 2.0 * math.sqrt(3.0 / (coords * n_param))

    def partner(o):
        return lax.rem(chip + o, chips)

    def fetch(s):
        return pltpu.make_async_copy(
            grads_ref.at[:, pl.ds(pl.multiple_of(s * slab, slab), slab)], stage.at[s], grad_sem.at[s]
        )

    for s in range(slabs):
        fetch(s).start()
    fetch_store = pltpu.make_async_copy(stored_ref, store, store_sem)
    fetch_store.start()

    barrier = pltpu.get_barrier_semaphore()
    pl.semaphore_signal(barrier, inc=1, device_id={"param": sibling}, device_id_type=MESH)
    for o in range(1, chips):
        pl.semaphore_signal(
            barrier, inc=1, device_id={"param": partner(o) * 2 + core}, device_id_type=MESH
        )
    for o in range(1, n_proj):
        pl.semaphore_signal(
            barrier, inc=1, device_id={"proj": lax.rem(here + o, n_proj)}, device_id_type=MESH
        )

    for n in range(chunks):
        at = pl.ds(n * chunk, chunk)
        shape = (16, chunk)
        column = here * width + n * chunk + lax.broadcasted_iota(jnp.int32, shape, 1)
        row = lax.broadcasted_iota(jnp.int32, shape, 0)
        start = reduced(jnp.full(shape, offset_ref[0] * 1103 + seed_ref[0], jnp.int32))
        factor = reduced(column * 2111 + seed_ref[1]) + 1
        slope = reduced(factor * 1103)
        level = reduced((start + 3) * factor + 14)
        square = reduced(slope * slope)
        linear = reduced(reduced(slope * level) * 2 + 1103)
        constant = reduced(level * level + start)
        weights = jnp.concatenate([weight_ref[...]] * (chunk // 128), axis=1)
        pair_coef = reduced(jnp.concatenate([square, square], axis=0) * weights)
        high, low = two_pieces(pair_coef.astype(jnp.float32))
        cross[pl.ds(0, 32), at] = high
        cross[pl.ds(32, 32), at] = low
        power = jnp.where(row < bits, jnp.left_shift(1, jnp.minimum(row, bits)), 0)
        first = reduced(reduced(square * power) * power + linear * power)
        first = jnp.where(row == bits, reduced(constant - middle), first)
        twice = reduced(square * (2 * block))
        step = reduced(twice * power)
        leap = reduced(reduced(square * block) * block + linear * block)
        step = jnp.where(row == bits, leap, step)
        bend = jnp.where(row == bits, reduced(twice * block), 0)
        bend = bend.astype(jnp.float32)

        def advance(i, state):
            value, step = state
            high, low = two_pieces(value)
            vary[i, pl.ds(0, 16), at] = high
            vary[i, pl.ds(16, 16), at] = low
            return reduced_float(value + step), reduced_float(step + bend)

        lax.fori_loop(
            0, coords // block, advance, (first.astype(jnp.float32), step.astype(jnp.float32))
        )

    @pl.loop(0, slabs)
    def _(s):
        fetch(s).wait()
        at = pl.ds(pl.multiple_of(s * slab, slab), slab)
        high, low = split(stage[s])
        high_q[:, at] = high
        low_q[:, at] = low

    def make(t, high, low):
        s = lax.rem(t, slabs)
        at = pl.ds(pl.multiple_of(lax.div(t, slabs) * chunk, chunk), chunk)
        blank = jnp.zeros((32, chunk), jnp.bfloat16)
        for b in range(slab_blocks):
            coef = jnp.concatenate([cross[:, at], vary[s * slab_blocks + b, :, at], blank], axis=0)
            x = mix(feat_ref[...], coef) * (1.0 / modulus)
            top, rest = split(x - jnp.round(x))
            high[pl.ds(b * block, block), :] = top
            low[pl.ds(b * block, block), :] = rest

    def use(t, high, low):
        s = lax.rem(t, slabs)
        at = pl.ds(pl.multiple_of(s * slab, slab), slab)
        qh = high_q[:, at]
        wh = high[...]
        total[...] += mix(qh, wh) + mix(low_q[:, at], wh) + mix(qh, low[...])

    def cols(n):
        return pl.ds(n * chunk, chunk)

    def pair_copy(n):
        return pltpu.make_async_remote_copy(
            src_ref=part.at[pl.ds(pl.multiple_of((1 - core) * half, half), half), cols(n)],
            dst_ref=pair_in.at[n], send_sem=pair_sem.at[0, n], recv_sem=pair_sem.at[1, n],
            device_id={"param": sibling}, device_id_type=MESH,
        )

    def ring_copy(n, o):
        to = partner(o)
        return pltpu.make_async_remote_copy(
            src_ref=part.at[pl.ds(pl.multiple_of(core * half + to * own, own), own), cols(n)],
            dst_ref=ring_in.at[n, o - 1],
            send_sem=ring_sem.at[0, n, o - 1], recv_sem=ring_sem.at[1, n, o - 1],
            device_id={"param": to * 2 + core}, device_id_type=MESH,
        )

    own_rows = pl.ds(pl.multiple_of(core * half + chip * own, own), own)
    half_rows = pl.ds(pl.multiple_of(core * half, half), half)

    def gather_copy(n, o):
        return pltpu.make_async_remote_copy(
            src_ref=proj.at[own_rows, cols(n)], dst_ref=proj.at[own_rows, cols(n)],
            send_sem=gather_sem.at[0, n, o - 1], recv_sem=gather_sem.at[1, n, o - 1],
            device_id={"param": partner(o) * 2 + core}, device_id_type=MESH,
        )

    def back_copy(n):
        return pltpu.make_async_remote_copy(
            src_ref=proj.at[half_rows, cols(n)], dst_ref=proj.at[half_rows, cols(n)],
            send_sem=back_sem.at[0, n], recv_sem=back_sem.at[1, n],
            device_id={"param": sibling}, device_id_type=MESH,
        )

    def begin(n):
        column = here * width + n * chunk + lax.broadcasted_iota(jnp.int32, (1, chunk), 1)
        gain = jnp.sqrt(1.0 + column.astype(jnp.float32) * (2.0 / width_total)) * scale
        part[:, cols(n)] = total[...] * gain
        pair_copy(n).start()

    def spread(n):
        pair_copy(n).wait_recv()
        part[half_rows, cols(n)] += pair_in[n]
        for o in range(1, chips):
            ring_copy(n, o).start()

    def join(n):
        value = part[own_rows, cols(n)]
        for o in range(1, chips):
            ring_copy(n, o).wait_recv()
            value += ring_in[n, o - 1]
        proj[own_rows, cols(n)] = value
        for o in range(1, chips):
            gather_copy(n, o).start()

    def hand_back(n):
        for o in range(1, chips):
            gather_copy(n, o).wait_recv()
        back_copy(n).start()

    def score(n):
        back_copy(n).wait_recv()
        value = proj[:, cols(n)]
        if n == 0:
            fetch_store.wait()
        high, low = split(value)
        squares = jnp.sum(value * value, axis=1, keepdims=True)
        squares = jnp.broadcast_to(squares, (queries, 128))
        column_sum[...] = squares if n == 0 else column_sum[...] + squares
        tile = min(store_rows, 256)
        for r in range(store_rows // tile):
            at = pl.ds(r * tile, tile)
            sh, sl = split(store[at, cols(n)])
            term = mix_rows(high, sh) + mix_rows(low, sh) + mix_rows(high, sl)
            raw[:, at] = term if n == 0 else raw[:, at] + term

    make(0, high_a, low_a)
    pl.semaphore_wait(barrier, n_param // 2 + n_proj - 1)

    for n in range(chunks):
        total[...] = jnp.zeros_like(total)
        for pair in range(slabs // 2):
            t = n * slabs + pair * 2
            make(t + 1, high_b, low_b)
            use(t, high_a, low_a)
            if t + 2 < chunks * slabs:
                make(t + 2, high_a, low_a)
            use(t + 1, high_b, low_b)
            if n > 0:
                if pair == 0:
                    spread(n - 1)
                if pair == slabs // 4:
                    join(n - 1)
                if pair == slabs // 2 - 1:
                    hand_back(n - 1)
            if n > 1 and pair == 1:
                score(n - 2)
        begin(n)
    last = chunks - 1
    spread(last)
    if chunks > 1:
        score(last - 1)
    join(last)
    hand_back(last)
    score(last)

    square_out[...] = column_sum[...].T[:8, :]

    def square_copy(o):
        return pltpu.make_async_remote_copy(
            src_ref=square_out, dst_ref=square_in.at[o - 1],
            send_sem=square_sem.at[0, o - 1], recv_sem=square_sem.at[1, o - 1],
            device_id={"proj": lax.rem(here + o, n_proj)}, device_id_type=MESH,
        )

    for o in range(1, n_proj):
        square_copy(o).start()

    def line_rows(goal, p):
        return pl.ds(pl.multiple_of(goal * share + p * piece, piece), piece)

    def line_copy(way, goal, p):
        return pltpu.make_async_remote_copy(
            src_ref=raw.at[line_rows(goal, p), :], dst_ref=line_in.at[way, goal, p],
            send_sem=line_sem.at[0, way, goal, p], recv_sem=line_sem.at[1, way, goal, p],
            device_id={"proj": lax.rem(here + 1 - 2 * way + n_proj, n_proj)}, device_id_type=MESH,
        )

    def arrived(way, goal, p):
        line_copy(way, goal, p).wait_recv()
        raw[line_rows(goal, p), :] += line_in[way, goal, p]

    late = (here >= (n_proj + 1) // 2).astype(jnp.int32)

    def moves(k, way):
        goal = (1 - way) * (n_proj - 1 - k) + way * k
        ahead = (goal - here) * (1 - 2 * way)
        behind = (1 - way) * here + way * (n_proj - 1 - here)
        return goal, ahead, behind

    for k in range(n_proj - 1):
        for p in range(pieces):
            for order in range(2):
                way = late + order - 2 * late * order
                goal, ahead, behind = moves(k, way)

                @pl.when(ahead > 0)
                def _():
                    @pl.when(behind > 0)
                    def _():
                        arrived(way, goal, p)

                    line_copy(way, goal, p).start()

    whole = column_sum[...].T[:8, :]
    for o in range(1, n_proj):
        square_copy(o).wait_recv()
        whole += square_in[o - 1]
    inverse = lax.rsqrt(whole * (1.0 / width_total) + epsilon) * (1.0 / math.sqrt(width_total))
    column_sum[...] = jnp.broadcast_to(inverse[:1, :], (128, queries)).T
    for p in range(pieces):
        @pl.when(here > 0)
        def _():
            arrived(0, here, p)

        @pl.when(here < n_proj - 1)
        def _():
            arrived(1, here, p)

        rows = line_rows(here, p)
        factor = column_sum[rows, :][:, :1]
        out_ref[pl.ds(p * piece, piece), :] = jnp.tanh(raw[rows, :] * factor)

    for n in range(chunks):
        pair_copy(n).wait_send()
        back_copy(n).wait_send()
        for o in range(1, chips):
            ring_copy(n, o).wait_send()
            gather_copy(n, o).wait_send()
    for o in range(1, n_proj):
        square_copy(o).wait_send()
    for k in range(n_proj - 1):
        for p in range(pieces):
            for way in range(2):
                goal, ahead, behind = moves(k, way)

                @pl.when(ahead > 0)
                def _():
                    line_copy(way, goal, p).wait_send()


def on_device(query_grads, stored, proj_seed, offsets):
    n_param = lax.axis_size("param")
    n_proj = lax.axis_size("proj")
    queries, coords = query_grads.shape
    store_rows, width = stored.shape
    chips = n_param // 2
    chunks = width // chunk
    slabs = coords // slab
    share = queries // n_proj
    own = queries // n_param
    vmem = pl.BlockSpec(memory_space=pltpu.VMEM)
    smem = pl.BlockSpec(memory_space=pltpu.SMEM)
    hbm = pl.BlockSpec(memory_space=pl.ANY)
    weight = pltpu.VMEM((slab, chunk), jnp.bfloat16)
    dma = pltpu.SemaphoreType.DMA
    return pl.pallas_call(
        functools.partial(kernel, n_param, n_proj),
        out_shape=jax.ShapeDtypeStruct((share, store_rows), jnp.float32),
        in_specs=[smem, smem, vmem, vmem, hbm, hbm],
        out_specs=vmem,
        scratch_shapes=[
            pltpu.VMEM((slabs, queries, slab), jnp.float32),
            pltpu.VMEM((store_rows, width), jnp.float32),
            pltpu.VMEM((queries, coords), jnp.bfloat16),
            pltpu.VMEM((queries, coords), jnp.bfloat16),
            pltpu.VMEM((64, width), jnp.bfloat16),
            pltpu.VMEM((coords // block, 32, width), jnp.bfloat16),
            weight, weight, weight, weight,
            pltpu.VMEM((queries, chunk), jnp.float32),
            pltpu.VMEM((queries, width), jnp.float32),
            pltpu.VMEM((chunks, queries // 2, chunk), jnp.float32),
            pltpu.VMEM((chunks, chips - 1, own, chunk), jnp.float32),
            pltpu.VMEM((queries, width), jnp.float32),
            pltpu.VMEM((queries, store_rows), jnp.float32),
            pltpu.VMEM((8, queries), jnp.float32),
            pltpu.VMEM((n_proj - 1, 8, queries), jnp.float32),
            pltpu.VMEM((queries, 128), jnp.float32),
            pltpu.VMEM((2, n_proj, pieces, share // pieces, store_rows), jnp.float32),
            dma((slabs,)),
            dma,
            dma((2, chunks)),
            dma((2, chunks, chips - 1)),
            dma((2, chunks, chips - 1)),
            dma((2, chunks)),
            dma((2, n_proj - 1)),
            dma((2, 2, n_proj, pieces)),
        ],
        compiler_params=pltpu.CompilerParams(
            collective_id=0, has_side_effects=True, vmem_limit_bytes=58 * 1024 * 1024
        ),
        name="attribution",
    )(offsets, proj_seed, bit_features(), pair_weights(), query_grads, stored)


def solution(mesh):
    placed = (P(None, "param"), P("param", "proj"), P(), P("param"))
    return jax.shard_map(
        on_device, mesh=mesh, in_specs=placed, out_specs=P("proj", "param"), check_vma=False
    )
```

```python
import functools
import math

import jax
import jax.numpy as jnp
import numpy as np
from jax import lax
from jax.experimental import pallas as pl
from jax.experimental.pallas import tpu as pltpu
from jax.sharding import PartitionSpec as P

modulus = 32749
middle = modulus // 2
epsilon = 1e-06
bits = 8
block = 1 << bits
pairs = [(p, q) for p in range(bits) for q in range(p + 1, bits)]
slab_blocks = 4
slab = block * slab_blocks
chunk = 256
MESH = pl.DeviceIdType.MESH


def bit_features():
    digits = (np.arange(block)[:, None] >> np.arange(bits)[None, :]) & 1
    cross = np.stack([digits[:, p] * digits[:, q] for p, q in pairs], axis=1)
    vary = np.concatenate([digits, np.ones((block, 1), digits.dtype)], axis=1)
    out = np.zeros((block, 128), np.float32)
    for at in (0, 32):
        out[:, at : at + len(pairs)] = cross
    for at in (64, 80):
        out[:, at : at + bits + 1] = vary
    return jnp.asarray(out, jnp.bfloat16)


def pair_weights():
    out = np.zeros((32, 128), np.int32)
    for row, (p, q) in enumerate(pairs):
        out[row] = 2 ** (p + q + 1)
    return jnp.asarray(out)


def reduced(value):
    times = jnp.round(value.astype(jnp.float32) * (1.0 / modulus)).astype(jnp.int32)
    return value - times * modulus


def reduced_float(value):
    return value - jnp.round(value * (1.0 / modulus)) * modulus


def two_pieces(value):
    high = jnp.round(value * (1.0 / 128)) * 128.0
    return high.astype(jnp.bfloat16), (value - high).astype(jnp.bfloat16)


def split(value):
    high = value.astype(jnp.bfloat16)
    return high, (value - high.astype(jnp.float32)).astype(jnp.bfloat16)


def mix(a, b):
    return jnp.dot(a, b, preferred_element_type=jnp.float32)


def mix_rows(a, b):
    return lax.dot_general(a, b, (((1,), (1,)), ((), ())), preferred_element_type=jnp.float32)


def kernel(n_param, n_proj, offset_ref, seed_ref, feat_ref, weight_ref, grads_ref, stored_ref, out_ref,
           stage, store, high_q, low_q, cross, vary, high_a, low_a, high_b, low_b, total,
           part, pair_in, ring_in, proj, raw, square_out, square_in, column_sum, line_in, state, score_high, score_low,
           grad_sem, store_sem, pair_sem, ring_sem, gather_sem, back_sem, square_sem, line_sem):
    queries, coords = high_q.shape
    store_rows, width = store.shape
    slabs = coords // slab
    chunks = width // chunk
    chips = n_param // 2
    half = queries // 2
    own = half // chips
    share = queries // n_proj
    tile = min(store_rows, 256)
    tiles = store_rows // tile
    me = lax.axis_index("param")
    here = lax.axis_index("proj")
    core = lax.rem(me, 2)
    chip = lax.div(me, 2)
    sibling = me + 1 - 2 * core
    width_total = width * n_proj
    scale = 2.0 * math.sqrt(3.0 / (coords * n_param))

    def partner(o):
        return lax.rem(chip + o, chips)

    def fetch(s):
        return pltpu.make_async_copy(
            grads_ref.at[:, pl.ds(pl.multiple_of(s * slab, slab), slab)], stage.at[s], grad_sem.at[s]
        )

    for s in range(slabs):
        fetch(s).start()
    fetch_store = pltpu.make_async_copy(stored_ref, store, store_sem)
    fetch_store.start()

    barrier = pltpu.get_barrier_semaphore()
    pl.semaphore_signal(barrier, inc=1, device_id={"param": sibling}, device_id_type=MESH)
    for o in range(1, chips):
        pl.semaphore_signal(
            barrier, inc=1, device_id={"param": partner(o) * 2 + core}, device_id_type=MESH
        )
    for o in range(1, n_proj):
        pl.semaphore_signal(
            barrier, inc=1, device_id={"proj": lax.rem(here + o, n_proj)}, device_id_type=MESH
        )

    shape = (16, width)
    column = here * width + lax.broadcasted_iota(jnp.int32, shape, 1)
    row = lax.broadcasted_iota(jnp.int32, shape, 0)
    start = reduced(jnp.full(shape, offset_ref[0] * 1103 + seed_ref[0], jnp.int32))
    factor = reduced(column * 2111 + seed_ref[1]) + 1
    slope = reduced(factor * 1103)
    level = reduced((start + 3) * factor + 14)
    square = reduced(slope * slope)
    linear = reduced(reduced(slope * level) * 2 + 1103)
    constant = reduced(level * level + start)
    weights = jnp.concatenate([weight_ref[...]] * (width // 128), axis=1)
    pair_coef = reduced(jnp.concatenate([square, square], axis=0) * weights)
    high, low = two_pieces(pair_coef.astype(jnp.float32))
    cross[pl.ds(0, 32), :] = high
    cross[pl.ds(32, 32), :] = low
    power = jnp.where(row < bits, jnp.left_shift(1, jnp.minimum(row, bits)), 0)
    first = reduced(reduced(square * power) * power + linear * power)
    first = jnp.where(row == bits, reduced(constant - middle), first)
    twice = reduced(square * (2 * block))
    step = reduced(twice * power)
    leap = reduced(reduced(square * block) * block + linear * block)
    step = jnp.where(row == bits, leap, step)
    bend = jnp.where(row == bits, reduced(twice * block), 0)
    state[0] = first.astype(jnp.float32)
    state[1] = step.astype(jnp.float32)
    state[2] = bend.astype(jnp.float32)

    @pl.loop(0, coords // block)
    def _(i):
        value = state[0]
        step = state[1]
        high, low = two_pieces(value)
        vary[i, pl.ds(0, 16), :] = high
        vary[i, pl.ds(16, 16), :] = low
        state[0] = reduced_float(value + step)
        state[1] = reduced_float(step + state[2])

    def prepare(s):
        fetch(s).wait()
        at = pl.ds(pl.multiple_of(s * slab, slab), slab)
        high, low = split(stage[s])
        high_q[:, at] = high
        low_q[:, at] = low

    def make(t, high, low):
        s = lax.rem(t, slabs)
        at = pl.ds(pl.multiple_of(lax.div(t, slabs) * chunk, chunk), chunk)
        blank = jnp.zeros((32, chunk), jnp.bfloat16)
        for b in range(slab_blocks):
            coef = jnp.concatenate([cross[:, at], vary[s * slab_blocks + b, :, at], blank], axis=0)
            x = mix(feat_ref[...], coef) * (1.0 / modulus)
            top, rest = split(x - jnp.round(x))
            high[pl.ds(b * block, block), :] = top
            low[pl.ds(b * block, block), :] = rest

    def use(t, high, low):
        s = lax.rem(t, slabs)
        at = pl.ds(pl.multiple_of(s * slab, slab), slab)
        qh = high_q[:, at]
        wh = high[...]
        total[...] += mix(qh, wh) + mix(low_q[:, at], wh) + mix(qh, low[...])

    def cols(n):
        return pl.ds(pl.multiple_of(n * chunk, chunk), chunk)

    def pair_copy(n):
        return pltpu.make_async_remote_copy(
            src_ref=part.at[pl.ds(pl.multiple_of((1 - core) * half, half), half), cols(n)],
            dst_ref=pair_in.at[n], send_sem=pair_sem.at[0, n], recv_sem=pair_sem.at[1, n],
            device_id={"param": sibling}, device_id_type=MESH,
        )

    def ring_copy(n, o):
        to = partner(o)
        return pltpu.make_async_remote_copy(
            src_ref=part.at[pl.ds(pl.multiple_of(core * half + to * own, own), own), cols(n)],
            dst_ref=ring_in.at[n, o - 1],
            send_sem=ring_sem.at[0, n, o - 1], recv_sem=ring_sem.at[1, n, o - 1],
            device_id={"param": to * 2 + core}, device_id_type=MESH,
        )

    own_rows = pl.ds(pl.multiple_of(core * half + chip * own, own), own)
    half_rows = pl.ds(pl.multiple_of(core * half, half), half)

    def gather_copy(n, o):
        return pltpu.make_async_remote_copy(
            src_ref=proj.at[own_rows, cols(n)], dst_ref=proj.at[own_rows, cols(n)],
            send_sem=gather_sem.at[0, n, o - 1], recv_sem=gather_sem.at[1, n, o - 1],
            device_id={"param": partner(o) * 2 + core}, device_id_type=MESH,
        )

    def back_copy(n):
        return pltpu.make_async_remote_copy(
            src_ref=proj.at[half_rows, cols(n)], dst_ref=proj.at[half_rows, cols(n)],
            send_sem=back_sem.at[0, n], recv_sem=back_sem.at[1, n],
            device_id={"param": sibling}, device_id_type=MESH,
        )

    def begin(n):
        column = here * width + n * chunk + lax.broadcasted_iota(jnp.int32, (1, chunk), 1)
        gain = jnp.sqrt(1.0 + column.astype(jnp.float32) * (2.0 / width_total)) * scale
        part[:, cols(n)] = total[...] * gain
        total[...] = jnp.zeros_like(total)
        pair_copy(n).start()

    def spread(n):
        pair_copy(n).wait_recv()
        part[half_rows, cols(n)] += pair_in[n]
        for o in range(1, chips):
            ring_copy(n, o).start()

    def join(n):
        value = part[own_rows, cols(n)]
        for o in range(1, chips):
            ring_copy(n, o).wait_recv()
            value += ring_in[n, o - 1]
        proj[own_rows, cols(n)] = value
        for o in range(1, chips):
            gather_copy(n, o).start()

    def hand_back(n):
        for o in range(1, chips):
            gather_copy(n, o).wait_recv()
        back_copy(n).start()

    def sums(n):
        back_copy(n).wait_recv()
        value = proj[:, cols(n)]
        high, low = split(value)
        score_high[...] = high
        score_low[...] = low
        squares = jnp.sum(value * value, axis=1, keepdims=True)
        column_sum[...] += jnp.broadcast_to(squares, (queries, 128))

    def score(n, r):
        at = pl.ds(pl.multiple_of(r * tile, tile), tile)
        sh, sl = split(store[at, cols(n)])
        high = score_high[...]
        raw[:, at] += mix_rows(high, sh) + mix_rows(score_low[...], sh) + mix_rows(high, sl)

    def scores(n):
        sums(n)

        @pl.loop(0, tiles)
        def _(r):
            score(n, r)

    def square_copy(o):
        return pltpu.make_async_remote_copy(
            src_ref=square_out, dst_ref=square_in.at[o - 1],
            send_sem=square_sem.at[0, o - 1], recv_sem=square_sem.at[1, o - 1],
            device_id={"proj": lax.rem(here + o, n_proj)}, device_id_type=MESH,
        )

    def piece(goal, p):
        return (
            pl.ds(pl.multiple_of(goal * share, share), share),
            pl.ds(pl.multiple_of(p * tile, tile), tile),
        )

    def line_copy(way, goal, p):
        return pltpu.make_async_remote_copy(
            src_ref=raw.at[piece(goal, p)], dst_ref=line_in.at[way, goal, p],
            send_sem=line_sem.at[0, way, goal, p], recv_sem=line_sem.at[1, way, goal, p],
            device_id={"proj": lax.rem(here + 1 - 2 * way + n_proj, n_proj)}, device_id_type=MESH,
        )

    def arrived(way, goal, p):
        line_copy(way, goal, p).wait_recv()
        raw[piece(goal, p)] += line_in[way, goal, p]

    late = (here >= (n_proj + 1) // 2).astype(jnp.int32)

    def moves(k, way):
        goal = (1 - way) * (n_proj - 1 - k) + way * k
        ahead = (goal - here) * (1 - 2 * way)
        behind = (1 - way) * here + way * (n_proj - 1 - here)
        return goal, ahead, behind

    total[...] = jnp.zeros_like(total)
    raw[...] = jnp.zeros_like(raw)
    column_sum[...] = jnp.zeros_like(column_sum)
    make(0, high_a, low_a)
    pl.semaphore_wait(barrier, n_param // 2 + n_proj - 1)
    turns = slabs // 2

    @pl.loop(0, chunks * turns)
    def _(it):
        t = it * 2

        @pl.when(it < turns)
        def _():
            prepare(t)
            prepare(t + 1)

        make(t + 1, high_b, low_b)
        use(t, high_a, low_a)
        make(jnp.minimum(t + 2, chunks * slabs - 1), high_a, low_a)
        use(t + 1, high_b, low_b)

        def after(delay, stage_of):
            turn = it - delay - (turns - 1)

            @pl.when((turn >= 0) & (lax.rem(turn + turns, turns) == 0))
            def _():
                stage_of(lax.div(turn, turns))

        after(0, begin)
        after(1, spread)
        after(3, join)
        after(4, hand_back)

        @pl.when(it == turns + 1)
        def _():
            fetch_store.wait()

        after(6, scores)

    last = chunks - 1
    spread(last)
    scores(last - 1)
    join(last)
    hand_back(last)
    sums(last)

    square_out[...] = column_sum[...].T[:8, :]
    for o in range(1, n_proj):
        square_copy(o).start()

    @pl.loop(0, tiles)
    def _(p):
        score(last, p)

        @pl.loop(0, n_proj - 1)
        def _(k):
            for way in range(2):
                goal, ahead, behind = moves(k, way)

                @pl.when((behind == 0) & (ahead > 0))
                def _():
                    line_copy(way, goal, p).start()

    @pl.loop(0, tiles)
    def _(p):
        @pl.loop(0, n_proj - 1)
        def _(k):
            for order in range(2):
                way = late + order - 2 * late * order
                goal, ahead, behind = moves(k, way)

                @pl.when((ahead > 0) & (behind > 0))
                def _():
                    arrived(way, goal, p)
                    line_copy(way, goal, p).start()

    whole = column_sum[...].T[:8, :]
    for o in range(1, n_proj):
        square_copy(o).wait_recv()
        whole += square_in[o - 1]
    inverse = lax.rsqrt(whole * (1.0 / width_total) + epsilon) * (1.0 / math.sqrt(width_total))
    column_sum[...] = jnp.broadcast_to(inverse[:1, :], (128, queries)).T

    @pl.loop(0, tiles)
    def _(p):
        @pl.when(here > 0)
        def _():
            arrived(0, here, p)

        @pl.when(here < n_proj - 1)
        def _():
            arrived(1, here, p)

        rows, at = piece(here, p)
        out_ref[:, at] = jnp.tanh(raw[rows, at] * column_sum[rows, :][:, :1])

    @pl.loop(0, chunks)
    def _(n):
        pair_copy(n).wait_send()
        back_copy(n).wait_send()
        for o in range(1, chips):
            ring_copy(n, o).wait_send()
            gather_copy(n, o).wait_send()

    for o in range(1, n_proj):
        square_copy(o).wait_send()

    @pl.loop(0, tiles)
    def _(p):
        @pl.loop(0, n_proj - 1)
        def _(k):
            for way in range(2):
                goal, ahead, behind = moves(k, way)

                @pl.when(ahead > 0)
                def _():
                    line_copy(way, goal, p).wait_send()


def on_device(query_grads, stored, proj_seed, offsets):
    n_param = lax.axis_size("param")
    n_proj = lax.axis_size("proj")
    queries, coords = query_grads.shape
    store_rows, width = stored.shape
    chips = n_param // 2
    chunks = width // chunk
    slabs = coords // slab
    share = queries // n_proj
    own = queries // n_param
    tile = min(store_rows, 256)
    tiles = store_rows // tile
    vmem = pl.BlockSpec(memory_space=pltpu.VMEM)
    smem = pl.BlockSpec(memory_space=pltpu.SMEM)
    hbm = pl.BlockSpec(memory_space=pl.ANY)
    weight = pltpu.VMEM((slab, chunk), jnp.bfloat16)
    dma = pltpu.SemaphoreType.DMA
    return pl.pallas_call(
        functools.partial(kernel, n_param, n_proj),
        out_shape=jax.ShapeDtypeStruct((share, store_rows), jnp.float32),
        in_specs=[smem, smem, vmem, vmem, hbm, hbm],
        out_specs=vmem,
        scratch_shapes=[
            pltpu.VMEM((slabs, queries, slab), jnp.float32),
            pltpu.VMEM((store_rows, width), jnp.float32),
            pltpu.VMEM((queries, coords), jnp.bfloat16),
            pltpu.VMEM((queries, coords), jnp.bfloat16),
            pltpu.VMEM((64, width), jnp.bfloat16),
            pltpu.VMEM((coords // block, 32, width), jnp.bfloat16),
            weight, weight, weight, weight,
            pltpu.VMEM((queries, chunk), jnp.float32),
            pltpu.VMEM((queries, width), jnp.float32),
            pltpu.VMEM((chunks, queries // 2, chunk), jnp.float32),
            pltpu.VMEM((chunks, chips - 1, own, chunk), jnp.float32),
            pltpu.VMEM((queries, width), jnp.float32),
            pltpu.VMEM((queries, store_rows), jnp.float32),
            pltpu.VMEM((8, queries), jnp.float32),
            pltpu.VMEM((n_proj - 1, 8, queries), jnp.float32),
            pltpu.VMEM((queries, 128), jnp.float32),
            pltpu.VMEM((2, n_proj, tiles, share, tile), jnp.float32),
            pltpu.VMEM((3, 16, width), jnp.float32),
            pltpu.VMEM((queries, chunk), jnp.bfloat16),
            pltpu.VMEM((queries, chunk), jnp.bfloat16),
            dma((slabs,)),
            dma,
            dma((2, chunks)),
            dma((2, chunks, chips - 1)),
            dma((2, chunks, chips - 1)),
            dma((2, chunks)),
            dma((2, n_proj - 1)),
            dma((2, 2, n_proj, tiles)),
        ],
        compiler_params=pltpu.CompilerParams(
            collective_id=0, has_side_effects=True, vmem_limit_bytes=58 * 1024 * 1024
        ),
        name="attribution",
    )(offsets, proj_seed, bit_features(), pair_weights(), query_grads, stored)


def solution(mesh):
    placed = (P(None, "param"), P("param", "proj"), P(), P("param"))
    return jax.shard_map(
        on_device, mesh=mesh, in_specs=placed, out_specs=P("proj", "param"), check_vma=False
    )
```

```python
import functools
import math

import jax
import jax.numpy as jnp
import numpy as np
from jax import lax
from jax.experimental import pallas as pl
from jax.experimental.pallas import tpu as pltpu
from jax.sharding import PartitionSpec as P

modulus = 32749
middle = modulus // 2
epsilon = 1e-06
bits = 8
block = 1 << bits
pairs = [(p, q) for p in range(bits) for q in range(p + 1, bits)]
slab_blocks = 4
slab = block * slab_blocks
chunk = 256
MESH = pl.DeviceIdType.MESH


def bit_features():
    digits = (np.arange(block)[:, None] >> np.arange(bits)[None, :]) & 1
    cross = np.stack([digits[:, p] * digits[:, q] for p, q in pairs], axis=1)
    vary = np.concatenate([digits, np.ones((block, 1), digits.dtype)], axis=1)
    out = np.zeros((block, 128), np.float32)
    for at in (0, 32):
        out[:, at : at + len(pairs)] = cross
    for at in (64, 80):
        out[:, at : at + bits + 1] = vary
    return jnp.asarray(out, jnp.bfloat16)


def pair_weights():
    out = np.zeros((32, 128), np.int32)
    for row, (p, q) in enumerate(pairs):
        out[row] = 2 ** (p + q + 1)
    return jnp.asarray(out)


def reduced(value):
    times = jnp.round(value.astype(jnp.float32) * (1.0 / modulus)).astype(jnp.int32)
    return value - times * modulus


def reduced_float(value):
    return value - jnp.round(value * (1.0 / modulus)) * modulus


def two_pieces(value):
    high = jnp.round(value * (1.0 / 128)) * 128.0
    return high.astype(jnp.bfloat16), (value - high).astype(jnp.bfloat16)


def split(value):
    high = value.astype(jnp.bfloat16)
    return high, (value - high.astype(jnp.float32)).astype(jnp.bfloat16)


def mix(a, b):
    return jnp.dot(a, b, preferred_element_type=jnp.float32)


def mix_rows(a, b):
    return lax.dot_general(a, b, (((1,), (1,)), ((), ())), preferred_element_type=jnp.float32)


def kernel(n_param, n_proj, offset_ref, seed_ref, feat_ref, weight_ref, grads_ref, stored_ref, out_ref,
           stage, store, high_q, low_q, cross, vary, high_a, low_a, high_b, low_b, total,
           part, pair_in, ring_in, proj, raw, square_out, square_in, column_sum, line_in, state, score_high, score_low,
           grad_sem, store_sem, pair_sem, ring_sem, gather_sem, back_sem, square_sem, line_sem):
    queries, coords = high_q.shape
    store_rows, width = store.shape
    slabs = coords // slab
    chunks = width // chunk
    chips = n_param // 2
    half = queries // 2
    own = half // chips
    share = queries // n_proj
    tile = min(store_rows, 256)
    tiles = store_rows // tile
    me = lax.axis_index("param")
    here = lax.axis_index("proj")
    core = lax.rem(me, 2)
    chip = lax.div(me, 2)
    sibling = me + 1 - 2 * core
    width_total = width * n_proj
    scale = 2.0 * math.sqrt(3.0 / (coords * n_param))

    def partner(o):
        return lax.rem(chip + o, chips)

    def fetch(s):
        return pltpu.make_async_copy(
            grads_ref.at[:, pl.ds(pl.multiple_of(s * slab, slab), slab)], stage.at[s], grad_sem.at[s]
        )

    for s in range(slabs):
        fetch(s).start()
    fetch_store = pltpu.make_async_copy(stored_ref, store, store_sem)
    fetch_store.start()

    barrier = pltpu.get_barrier_semaphore()
    pl.semaphore_signal(barrier, inc=1, device_id={"param": sibling}, device_id_type=MESH)
    for o in range(1, chips):
        pl.semaphore_signal(
            barrier, inc=1, device_id={"param": partner(o) * 2 + core}, device_id_type=MESH
        )
    for o in range(1, n_proj):
        pl.semaphore_signal(
            barrier, inc=1, device_id={"proj": lax.rem(here + o, n_proj)}, device_id_type=MESH
        )

    shape = (16, width)
    column = here * width + lax.broadcasted_iota(jnp.int32, shape, 1)
    row = lax.broadcasted_iota(jnp.int32, shape, 0)
    start = reduced(jnp.full(shape, offset_ref[0] * 1103 + seed_ref[0], jnp.int32))
    factor = reduced(column * 2111 + seed_ref[1]) + 1
    slope = reduced(factor * 1103)
    level = reduced((start + 3) * factor + 14)
    square = reduced(slope * slope)
    linear = reduced(reduced(slope * level) * 2 + 1103)
    constant = reduced(level * level + start)
    weights = jnp.concatenate([weight_ref[...]] * (width // 128), axis=1)
    pair_coef = reduced(jnp.concatenate([square, square], axis=0) * weights)
    high, low = two_pieces(pair_coef.astype(jnp.float32))
    cross[pl.ds(0, 32), :] = high
    cross[pl.ds(32, 32), :] = low
    power = jnp.where(row < bits, jnp.left_shift(1, jnp.minimum(row, bits)), 0)
    first = reduced(reduced(square * power) * power + linear * power)
    first = jnp.where(row == bits, reduced(constant - middle), first)
    twice = reduced(square * (2 * block))
    step = reduced(twice * power)
    leap = reduced(reduced(square * block) * block + linear * block)
    step = jnp.where(row == bits, leap, step)
    bend = jnp.where(row == bits, reduced(twice * block), 0)
    state[0] = first.astype(jnp.float32)
    state[1] = step.astype(jnp.float32)
    state[2] = bend.astype(jnp.float32)

    @pl.loop(0, coords // block)
    def _(i):
        value = state[0]
        step = state[1]
        high, low = two_pieces(value)
        vary[i, pl.ds(0, 16), :] = high
        vary[i, pl.ds(16, 16), :] = low
        state[0] = reduced_float(value + step)
        state[1] = reduced_float(step + state[2])

    def prepare(s):
        fetch(s).wait()
        at = pl.ds(pl.multiple_of(s * slab, slab), slab)
        high, low = split(stage[s])
        high_q[:, at] = high
        low_q[:, at] = low

    def make(t, high, low):
        s = lax.rem(t, slabs)
        at = pl.ds(pl.multiple_of(lax.div(t, slabs) * chunk, chunk), chunk)
        blank = jnp.zeros((32, chunk), jnp.bfloat16)
        for b in range(slab_blocks):
            coef = jnp.concatenate([cross[:, at], vary[s * slab_blocks + b, :, at], blank], axis=0)
            x = mix(feat_ref[...], coef) * (1.0 / modulus)
            top, rest = split(x - jnp.round(x))
            high[pl.ds(b * block, block), :] = top
            low[pl.ds(b * block, block), :] = rest

    def use(t, high, low):
        s = lax.rem(t, slabs)
        at = pl.ds(pl.multiple_of(s * slab, slab), slab)
        qh = high_q[:, at]
        wh = high[...]
        total[...] += mix(qh, wh) + mix(low_q[:, at], wh) + mix(qh, low[...])

    def cols(n):
        return pl.ds(pl.multiple_of(n * chunk, chunk), chunk)

    def pair_copy(n):
        return pltpu.make_async_remote_copy(
            src_ref=part.at[pl.ds(pl.multiple_of((1 - core) * half, half), half), cols(n)],
            dst_ref=pair_in.at[n], send_sem=pair_sem.at[0, n], recv_sem=pair_sem.at[1, n],
            device_id={"param": sibling}, device_id_type=MESH,
        )

    def ring_copy(n, o):
        to = partner(o)
        return pltpu.make_async_remote_copy(
            src_ref=part.at[pl.ds(pl.multiple_of(core * half + to * own, own), own), cols(n)],
            dst_ref=ring_in.at[n, o - 1],
            send_sem=ring_sem.at[0, n, o - 1], recv_sem=ring_sem.at[1, n, o - 1],
            device_id={"param": to * 2 + core}, device_id_type=MESH,
        )

    own_rows = pl.ds(pl.multiple_of(core * half + chip * own, own), own)
    half_rows = pl.ds(pl.multiple_of(core * half, half), half)

    def gather_copy(n, o):
        return pltpu.make_async_remote_copy(
            src_ref=proj.at[own_rows, cols(n)], dst_ref=proj.at[own_rows, cols(n)],
            send_sem=gather_sem.at[0, n, o - 1], recv_sem=gather_sem.at[1, n, o - 1],
            device_id={"param": partner(o) * 2 + core}, device_id_type=MESH,
        )

    def back_copy(n):
        return pltpu.make_async_remote_copy(
            src_ref=proj.at[half_rows, cols(n)], dst_ref=proj.at[half_rows, cols(n)],
            send_sem=back_sem.at[0, n], recv_sem=back_sem.at[1, n],
            device_id={"param": sibling}, device_id_type=MESH,
        )

    def begin(n):
        column = here * width + n * chunk + lax.broadcasted_iota(jnp.int32, (1, chunk), 1)
        gain = jnp.sqrt(1.0 + column.astype(jnp.float32) * (2.0 / width_total)) * scale
        part[:, cols(n)] = total[...] * gain
        total[...] = jnp.zeros_like(total)
        pair_copy(n).start()

    def spread(n):
        pair_copy(n).wait_recv()
        part[half_rows, cols(n)] += pair_in[n]
        for o in range(1, chips):
            ring_copy(n, o).start()

    def join(n):
        value = part[own_rows, cols(n)]
        for o in range(1, chips):
            ring_copy(n, o).wait_recv()
            value += ring_in[n, o - 1]
        proj[own_rows, cols(n)] = value
        for o in range(1, chips):
            gather_copy(n, o).start()

    def hand_back(n):
        for o in range(1, chips):
            gather_copy(n, o).wait_recv()
        back_copy(n).start()

    def sums(n):
        back_copy(n).wait_recv()
        value = proj[:, cols(n)]
        high, low = split(value)
        score_high[...] = high
        score_low[...] = low
        squares = jnp.sum(value * value, axis=1, keepdims=True)
        column_sum[...] += jnp.broadcast_to(squares, (queries, 128))

    def score(n, r):
        at = pl.ds(pl.multiple_of(r * tile, tile), tile)
        sh, sl = split(store[at, cols(n)])
        high = score_high[...]
        raw[:, at] += mix_rows(high, sh) + mix_rows(score_low[...], sh) + mix_rows(high, sl)

    def scores(n):
        sums(n)

        @pl.loop(0, tiles)
        def _(r):
            score(n, r)

    def square_copy(o):
        return pltpu.make_async_remote_copy(
            src_ref=square_out, dst_ref=square_in.at[o - 1],
            send_sem=square_sem.at[0, o - 1], recv_sem=square_sem.at[1, o - 1],
            device_id={"proj": lax.rem(here + o, n_proj)}, device_id_type=MESH,
        )

    def piece(goal, p):
        return (
            pl.ds(pl.multiple_of(goal * share, share), share),
            pl.ds(pl.multiple_of(p * tile, tile), tile),
        )

    def line_copy(way, goal, p):
        return pltpu.make_async_remote_copy(
            src_ref=raw.at[piece(goal, p)], dst_ref=line_in.at[way, goal, p],
            send_sem=line_sem.at[0, way, goal, p], recv_sem=line_sem.at[1, way, goal, p],
            device_id={"proj": lax.rem(here + 1 - 2 * way + n_proj, n_proj)}, device_id_type=MESH,
        )

    def arrived(way, goal, p):
        line_copy(way, goal, p).wait_recv()
        raw[piece(goal, p)] += line_in[way, goal, p]

    late = (here >= (n_proj + 1) // 2).astype(jnp.int32)

    def moves(k, way):
        goal = (1 - way) * (n_proj - 1 - k) + way * k
        ahead = (goal - here) * (1 - 2 * way)
        behind = (1 - way) * here + way * (n_proj - 1 - here)
        return goal, ahead, behind

    total[...] = jnp.zeros_like(total)
    raw[...] = jnp.zeros_like(raw)
    column_sum[...] = jnp.zeros_like(column_sum)
    make(0, high_a, low_a)
    pl.semaphore_wait(barrier, n_param // 2 + n_proj - 1)
    turns = slabs // 2

    @pl.loop(0, chunks * turns)
    def _(it):
        t = it * 2

        @pl.when(it < turns)
        def _():
            prepare(t)
            prepare(t + 1)

        make(t + 1, high_b, low_b)
        use(t, high_a, low_a)
        make(jnp.minimum(t + 2, chunks * slabs - 1), high_a, low_a)
        use(t + 1, high_b, low_b)

        def after(delay, stage_of):
            turn = it - delay - (turns - 1)

            @pl.when((turn >= 0) & (lax.rem(turn + turns, turns) == 0))
            def _():
                stage_of(lax.div(turn, turns))

        after(0, begin)
        after(1, spread)
        after(3, join)
        after(5, hand_back)

        @pl.when(it == turns + 1)
        def _():
            fetch_store.wait()

        after(7, scores)

    last = chunks - 1
    spread(last)
    hand_back(last - 1)
    scores(last - 1)
    join(last)
    hand_back(last)
    sums(last)

    square_out[...] = column_sum[...].T[:8, :]
    for o in range(1, n_proj):
        square_copy(o).start()

    @pl.loop(0, tiles)
    def _(p):
        score(last, p)

        @pl.loop(0, n_proj - 1)
        def _(k):
            for way in range(2):
                goal, ahead, behind = moves(k, way)

                @pl.when((behind == 0) & (ahead > 0))
                def _():
                    line_copy(way, goal, p).start()

    def forward(way, p):
        @pl.loop(0, n_proj - 1)
        def _(k):
            goal, ahead, behind = moves(k, way)

            @pl.when((ahead > 0) & (behind > 0))
            def _():
                arrived(way, goal, p)
                line_copy(way, goal, p).start()

    @pl.loop(0, tiles + 1)
    def _(p):
        @pl.when(p < tiles)
        def _():
            forward(late, p)

        @pl.when(p > 0)
        def _():
            forward(1 - late, p - 1)

    whole = column_sum[...].T[:8, :]
    for o in range(1, n_proj):
        square_copy(o).wait_recv()
        whole += square_in[o - 1]
    inverse = lax.rsqrt(whole * (1.0 / width_total) + epsilon) * (1.0 / math.sqrt(width_total))
    column_sum[...] = jnp.broadcast_to(inverse[:1, :], (128, queries)).T

    @pl.loop(0, tiles)
    def _(p):
        @pl.when(here > 0)
        def _():
            arrived(0, here, p)

        @pl.when(here < n_proj - 1)
        def _():
            arrived(1, here, p)

        rows, at = piece(here, p)
        out_ref[:, at] = jnp.tanh(raw[rows, at] * column_sum[rows, :][:, :1])

    @pl.loop(0, chunks)
    def _(n):
        pair_copy(n).wait_send()
        back_copy(n).wait_send()
        for o in range(1, chips):
            ring_copy(n, o).wait_send()
            gather_copy(n, o).wait_send()

    for o in range(1, n_proj):
        square_copy(o).wait_send()

    @pl.loop(0, tiles)
    def _(p):
        @pl.loop(0, n_proj - 1)
        def _(k):
            for way in range(2):
                goal, ahead, behind = moves(k, way)

                @pl.when(ahead > 0)
                def _():
                    line_copy(way, goal, p).wait_send()


def on_device(query_grads, stored, proj_seed, offsets):
    n_param = lax.axis_size("param")
    n_proj = lax.axis_size("proj")
    queries, coords = query_grads.shape
    store_rows, width = stored.shape
    chips = n_param // 2
    chunks = width // chunk
    slabs = coords // slab
    share = queries // n_proj
    own = queries // n_param
    tile = min(store_rows, 256)
    tiles = store_rows // tile
    vmem = pl.BlockSpec(memory_space=pltpu.VMEM)
    smem = pl.BlockSpec(memory_space=pltpu.SMEM)
    hbm = pl.BlockSpec(memory_space=pl.ANY)
    weight = pltpu.VMEM((slab, chunk), jnp.bfloat16)
    dma = pltpu.SemaphoreType.DMA
    return pl.pallas_call(
        functools.partial(kernel, n_param, n_proj),
        out_shape=jax.ShapeDtypeStruct((share, store_rows), jnp.float32),
        in_specs=[smem, smem, vmem, vmem, hbm, hbm],
        out_specs=vmem,
        scratch_shapes=[
            pltpu.VMEM((slabs, queries, slab), jnp.float32),
            pltpu.VMEM((store_rows, width), jnp.float32),
            pltpu.VMEM((queries, coords), jnp.bfloat16),
            pltpu.VMEM((queries, coords), jnp.bfloat16),
            pltpu.VMEM((64, width), jnp.bfloat16),
            pltpu.VMEM((coords // block, 32, width), jnp.bfloat16),
            weight, weight, weight, weight,
            pltpu.VMEM((queries, chunk), jnp.float32),
            pltpu.VMEM((queries, width), jnp.float32),
            pltpu.VMEM((chunks, queries // 2, chunk), jnp.float32),
            pltpu.VMEM((chunks, chips - 1, own, chunk), jnp.float32),
            pltpu.VMEM((queries, width), jnp.float32),
            pltpu.VMEM((queries, store_rows), jnp.float32),
            pltpu.VMEM((8, queries), jnp.float32),
            pltpu.VMEM((n_proj - 1, 8, queries), jnp.float32),
            pltpu.VMEM((queries, 128), jnp.float32),
            pltpu.VMEM((2, n_proj, tiles, share, tile), jnp.float32),
            pltpu.VMEM((3, 16, width), jnp.float32),
            pltpu.VMEM((queries, chunk), jnp.bfloat16),
            pltpu.VMEM((queries, chunk), jnp.bfloat16),
            dma((slabs,)),
            dma,
            dma((2, chunks)),
            dma((2, chunks, chips - 1)),
            dma((2, chunks, chips - 1)),
            dma((2, chunks)),
            dma((2, n_proj - 1)),
            dma((2, 2, n_proj, tiles)),
        ],
        compiler_params=pltpu.CompilerParams(
            collective_id=0, has_side_effects=True, vmem_limit_bytes=58 * 1024 * 1024
        ),
        name="attribution",
    )(offsets, proj_seed, bit_features(), pair_weights(), query_grads, stored)


def solution(mesh):
    placed = (P(None, "param"), P("param", "proj"), P(), P("param"))
    return jax.shard_map(
        on_device, mesh=mesh, in_specs=placed, out_specs=P("proj", "param"), check_vma=False
    )
```

```python
import functools
import math

import jax
import jax.numpy as jnp
import numpy as np
from jax import lax
from jax.experimental import pallas as pl
from jax.experimental.pallas import tpu as pltpu
from jax.sharding import PartitionSpec as P

modulus = 32749
middle = modulus // 2
epsilon = 1e-06
bits = 9
block = 1 << bits
pairs = [(p, q) for p in range(bits) for q in range(p + 1, bits)]
slab_blocks = 2
cross_rows = 48
slab = block * slab_blocks
chunk = 256
MESH = pl.DeviceIdType.MESH


def bit_features():
    digits = (np.arange(block)[:, None] >> np.arange(bits)[None, :]) & 1
    cross = np.stack([digits[:, p] * digits[:, q] for p, q in pairs], axis=1)
    vary = np.concatenate([digits, np.ones((block, 1), digits.dtype)], axis=1)
    out = np.zeros((block, 128), np.float32)
    for at in (0, cross_rows):
        out[:, at : at + len(pairs)] = cross
    for at in (2 * cross_rows, 2 * cross_rows + 16):
        out[:, at : at + bits + 1] = vary
    return jnp.asarray(out, jnp.bfloat16)


def pair_weights():
    out = np.zeros((cross_rows, 128), np.int32)
    for row, (p, q) in enumerate(pairs):
        out[row] = 2 ** (p + q + 1)
    return jnp.asarray(out)


def reduced(value):
    times = jnp.round(value.astype(jnp.float32) * (1.0 / modulus)).astype(jnp.int32)
    return value - times * modulus


def reduced_float(value):
    return value - jnp.round(value * (1.0 / modulus)) * modulus


def two_pieces(value):
    high = jnp.round(value * (1.0 / 128)) * 128.0
    return high.astype(jnp.bfloat16), (value - high).astype(jnp.bfloat16)


def split(value):
    high = value.astype(jnp.bfloat16)
    return high, (value - high.astype(jnp.float32)).astype(jnp.bfloat16)


def mix(a, b):
    return jnp.dot(a, b, preferred_element_type=jnp.float32)


def mix_rows(a, b):
    return lax.dot_general(a, b, (((1,), (1,)), ((), ())), preferred_element_type=jnp.float32)


def kernel(n_param, n_proj, offset_ref, seed_ref, feat_ref, weight_ref, grads_ref, stored_ref, out_ref,
           stage, store, both_q, cross, vary, high_a, low_a, high_b, low_b, total,
           part, pair_in, ring_in, proj, raw, square_out, square_in, column_sum, line_in, state, score_high, score_low,
           grad_sem, store_sem, pair_sem, ring_sem, gather_sem, back_sem, square_sem, line_sem):
    queries, coords = both_q.shape[0] // 2, both_q.shape[1]
    store_rows, width = store.shape
    slabs = coords // slab
    chunks = width // chunk
    chips = n_param // 2
    half = queries // 2
    own = half // chips
    share = queries // n_proj
    tile = min(store_rows, 256)
    tiles = store_rows // tile
    me = lax.axis_index("param")
    here = lax.axis_index("proj")
    core = lax.rem(me, 2)
    chip = lax.div(me, 2)
    sibling = me + 1 - 2 * core
    width_total = width * n_proj
    scale = 2.0 * math.sqrt(3.0 / (coords * n_param))

    def partner(o):
        return lax.rem(chip + o, chips)

    def fetch(s):
        return pltpu.make_async_copy(
            grads_ref.at[:, pl.ds(pl.multiple_of(s * slab, slab), slab)], stage.at[s], grad_sem.at[s]
        )

    for s in range(slabs):
        fetch(s).start()
    fetch_store = pltpu.make_async_copy(stored_ref, store, store_sem)
    fetch_store.start()

    barrier = pltpu.get_barrier_semaphore()
    pl.semaphore_signal(barrier, inc=1, device_id={"param": sibling}, device_id_type=MESH)
    for o in range(1, chips):
        pl.semaphore_signal(
            barrier, inc=1, device_id={"param": partner(o) * 2 + core}, device_id_type=MESH
        )
    for o in range(1, n_proj):
        pl.semaphore_signal(
            barrier, inc=1, device_id={"proj": lax.rem(here + o, n_proj)}, device_id_type=MESH
        )

    shape = (16, width)
    column = here * width + lax.broadcasted_iota(jnp.int32, shape, 1)
    row = lax.broadcasted_iota(jnp.int32, shape, 0)
    start = reduced(jnp.full(shape, offset_ref[0] * 1103 + seed_ref[0], jnp.int32))
    factor = reduced(column * 2111 + seed_ref[1]) + 1
    slope = reduced(factor * 1103)
    level = reduced((start + 3) * factor + 14)
    square = reduced(slope * slope)
    linear = reduced(reduced(slope * level) * 2 + 1103)
    constant = reduced(level * level + start)
    weights = jnp.concatenate([weight_ref[...]] * (width // 128), axis=1)
    pair_coef = reduced(jnp.concatenate([square] * (cross_rows // 16), axis=0) * weights)
    high, low = two_pieces(pair_coef.astype(jnp.float32))
    cross[pl.ds(0, cross_rows), :] = high
    cross[pl.ds(cross_rows, cross_rows), :] = low
    power = jnp.where(row < bits, jnp.left_shift(1, jnp.minimum(row, bits)), 0)
    first = reduced(reduced(square * power) * power + linear * power)
    first = jnp.where(row == bits, reduced(constant - middle), first)
    twice = reduced(square * (2 * block))
    step = reduced(twice * power)
    leap = reduced(reduced(square * block) * block + linear * block)
    step = jnp.where(row == bits, leap, step)
    bend = jnp.where(row == bits, reduced(twice * block), 0)
    state[0] = first.astype(jnp.float32)
    state[1] = step.astype(jnp.float32)
    state[2] = bend.astype(jnp.float32)

    @pl.loop(0, coords // block)
    def _(i):
        value = state[0]
        step = state[1]
        high, low = two_pieces(value)
        vary[i, pl.ds(0, 16), :] = high
        vary[i, pl.ds(16, 16), :] = low
        state[0] = reduced_float(value + step)
        state[1] = reduced_float(step + state[2])

    def prepare(s):
        fetch(s).wait()
        at = pl.ds(pl.multiple_of(s * slab, slab), slab)
        high, low = split(stage[s])
        both_q[pl.ds(0, queries), at] = high
        both_q[pl.ds(queries, queries), at] = low

    def make(t, high, low):
        s = lax.rem(t, slabs)
        at = pl.ds(pl.multiple_of(lax.div(t, slabs) * chunk, chunk), chunk)
        for b in range(slab_blocks):
            coef = jnp.concatenate([cross[:, at], vary[s * slab_blocks + b, :, at]], axis=0)
            x = mix(feat_ref[...], coef) * (1.0 / modulus)
            top, rest = split(x - jnp.round(x))
            high[pl.ds(b * block, block), :] = top
            low[pl.ds(b * block, block), :] = rest

    def use(t, high, low):
        s = lax.rem(t, slabs)
        at = pl.ds(pl.multiple_of(s * slab, slab), slab)
        main = mix(both_q[:, at], high[...])
        rest = mix(both_q[pl.ds(0, queries), at], low[...])
        total[...] += main[:queries] + (main[queries:] + rest)

    def cols(n):
        return pl.ds(pl.multiple_of(n * chunk, chunk), chunk)

    def pair_copy(n):
        return pltpu.make_async_remote_copy(
            src_ref=part.at[pl.ds(pl.multiple_of((1 - core) * half, half), half), cols(n)],
            dst_ref=pair_in.at[n], send_sem=pair_sem.at[0, n], recv_sem=pair_sem.at[1, n],
            device_id={"param": sibling}, device_id_type=MESH,
        )

    def ring_copy(n, o):
        to = partner(o)
        return pltpu.make_async_remote_copy(
            src_ref=part.at[pl.ds(pl.multiple_of(core * half + to * own, own), own), cols(n)],
            dst_ref=ring_in.at[n, o - 1],
            send_sem=ring_sem.at[0, n, o - 1], recv_sem=ring_sem.at[1, n, o - 1],
            device_id={"param": to * 2 + core}, device_id_type=MESH,
        )

    own_rows = pl.ds(pl.multiple_of(core * half + chip * own, own), own)
    half_rows = pl.ds(pl.multiple_of(core * half, half), half)

    def gather_copy(n, o):
        return pltpu.make_async_remote_copy(
            src_ref=proj.at[own_rows, cols(n)], dst_ref=proj.at[own_rows, cols(n)],
            send_sem=gather_sem.at[0, n, o - 1], recv_sem=gather_sem.at[1, n, o - 1],
            device_id={"param": partner(o) * 2 + core}, device_id_type=MESH,
        )

    def back_copy(n):
        return pltpu.make_async_remote_copy(
            src_ref=proj.at[half_rows, cols(n)], dst_ref=proj.at[half_rows, cols(n)],
            send_sem=back_sem.at[0, n], recv_sem=back_sem.at[1, n],
            device_id={"param": sibling}, device_id_type=MESH,
        )

    def begin(n):
        column = here * width + n * chunk + lax.broadcasted_iota(jnp.int32, (1, chunk), 1)
        gain = jnp.sqrt(1.0 + column.astype(jnp.float32) * (2.0 / width_total)) * scale
        part[:, cols(n)] = total[...] * gain
        total[...] = jnp.zeros_like(total)
        pair_copy(n).start()

    def spread(n):
        pair_copy(n).wait_recv()
        part[half_rows, cols(n)] += pair_in[n]
        for o in range(1, chips):
            ring_copy(n, o).start()

    def join(n):
        value = part[own_rows, cols(n)]
        for o in range(1, chips):
            ring_copy(n, o).wait_recv()
            value += ring_in[n, o - 1]
        proj[own_rows, cols(n)] = value
        for o in range(1, chips):
            gather_copy(n, o).start()

    def hand_back(n):
        for o in range(1, chips):
            gather_copy(n, o).wait_recv()
        back_copy(n).start()

    def sums(n):
        back_copy(n).wait_recv()
        value = proj[:, cols(n)]
        high, low = split(value)
        score_high[...] = high
        score_low[...] = low
        squares = jnp.sum(value * value, axis=1, keepdims=True)
        column_sum[...] += jnp.broadcast_to(squares, (queries, 128))

    def score(n, r):
        at = pl.ds(pl.multiple_of(r * tile, tile), tile)
        sh, sl = split(store[at, cols(n)])
        high = score_high[...]
        raw[:, at] += mix_rows(high, sh) + mix_rows(score_low[...], sh) + mix_rows(high, sl)

    def scores(n):
        sums(n)

        @pl.loop(0, tiles)
        def _(r):
            score(n, r)

    def square_copy(o):
        return pltpu.make_async_remote_copy(
            src_ref=square_out, dst_ref=square_in.at[o - 1],
            send_sem=square_sem.at[0, o - 1], recv_sem=square_sem.at[1, o - 1],
            device_id={"proj": lax.rem(here + o, n_proj)}, device_id_type=MESH,
        )

    def piece(goal, p):
        return (
            pl.ds(pl.multiple_of(goal * share, share), share),
            pl.ds(pl.multiple_of(p * tile, tile), tile),
        )

    def line_copy(way, goal, p):
        return pltpu.make_async_remote_copy(
            src_ref=raw.at[piece(goal, p)], dst_ref=line_in.at[way, goal, p],
            send_sem=line_sem.at[0, way, goal, p], recv_sem=line_sem.at[1, way, goal, p],
            device_id={"proj": lax.rem(here + 1 - 2 * way + n_proj, n_proj)}, device_id_type=MESH,
        )

    def arrived(way, goal, p):
        line_copy(way, goal, p).wait_recv()
        raw[piece(goal, p)] += line_in[way, goal, p]

    late = (here >= (n_proj + 1) // 2).astype(jnp.int32)

    def moves(k, way):
        goal = (1 - way) * (n_proj - 1 - k) + way * k
        ahead = (goal - here) * (1 - 2 * way)
        behind = (1 - way) * here + way * (n_proj - 1 - here)
        return goal, ahead, behind

    total[...] = jnp.zeros_like(total)
    raw[...] = jnp.zeros_like(raw)
    column_sum[...] = jnp.zeros_like(column_sum)
    make(0, high_a, low_a)
    pl.semaphore_wait(barrier, n_param // 2 + n_proj - 1)
    turns = slabs // 2

    @pl.loop(0, chunks * turns)
    def _(it):
        t = it * 2

        @pl.when(it < turns)
        def _():
            prepare(t)
            prepare(t + 1)

        make(t + 1, high_b, low_b)
        use(t, high_a, low_a)
        make(jnp.minimum(t + 2, chunks * slabs - 1), high_a, low_a)
        use(t + 1, high_b, low_b)

        def after(delay, stage_of):
            turn = it - delay - (turns - 1)

            @pl.when((turn >= 0) & (lax.rem(turn + turns, turns) == 0))
            def _():
                stage_of(lax.div(turn, turns))

        after(0, begin)
        after(1, spread)
        after(3, join)
        after(5, hand_back)

        @pl.when(it == turns + 1)
        def _():
            fetch_store.wait()

        after(7, scores)

    last = chunks - 1
    spread(last)
    hand_back(last - 1)
    scores(last - 1)
    join(last)
    hand_back(last)
    sums(last)

    square_out[...] = column_sum[...].T[:8, :]
    for o in range(1, n_proj):
        square_copy(o).start()

    @pl.loop(0, tiles)
    def _(p):
        score(last, p)

        @pl.loop(0, n_proj - 1)
        def _(k):
            for way in range(2):
                goal, ahead, behind = moves(k, way)

                @pl.when((behind == 0) & (ahead > 0))
                def _():
                    line_copy(way, goal, p).start()

    def forward(way, p):
        @pl.loop(0, n_proj - 1)
        def _(k):
            goal, ahead, behind = moves(k, way)

            @pl.when((ahead > 0) & (behind > 0))
            def _():
                arrived(way, goal, p)
                line_copy(way, goal, p).start()

    @pl.loop(0, tiles + 1)
    def _(p):
        @pl.when(p < tiles)
        def _():
            forward(late, p)

        @pl.when(p > 0)
        def _():
            forward(1 - late, p - 1)

    whole = column_sum[...].T[:8, :]
    for o in range(1, n_proj):
        square_copy(o).wait_recv()
        whole += square_in[o - 1]
    inverse = lax.rsqrt(whole * (1.0 / width_total) + epsilon) * (1.0 / math.sqrt(width_total))
    column_sum[...] = jnp.broadcast_to(inverse[:1, :], (128, queries)).T

    @pl.loop(0, tiles)
    def _(p):
        @pl.when(here > 0)
        def _():
            arrived(0, here, p)

        @pl.when(here < n_proj - 1)
        def _():
            arrived(1, here, p)

        rows, at = piece(here, p)
        out_ref[:, at] = jnp.tanh(raw[rows, at] * column_sum[rows, :][:, :1])

    @pl.loop(0, chunks)
    def _(n):
        pair_copy(n).wait_send()
        back_copy(n).wait_send()
        for o in range(1, chips):
            ring_copy(n, o).wait_send()
            gather_copy(n, o).wait_send()

    for o in range(1, n_proj):
        square_copy(o).wait_send()

    @pl.loop(0, tiles)
    def _(p):
        @pl.loop(0, n_proj - 1)
        def _(k):
            for way in range(2):
                goal, ahead, behind = moves(k, way)

                @pl.when(ahead > 0)
                def _():
                    line_copy(way, goal, p).wait_send()


def on_device(query_grads, stored, proj_seed, offsets):
    n_param = lax.axis_size("param")
    n_proj = lax.axis_size("proj")
    queries, coords = query_grads.shape
    store_rows, width = stored.shape
    chips = n_param // 2
    chunks = width // chunk
    slabs = coords // slab
    share = queries // n_proj
    own = queries // n_param
    tile = min(store_rows, 256)
    tiles = store_rows // tile
    vmem = pl.BlockSpec(memory_space=pltpu.VMEM)
    smem = pl.BlockSpec(memory_space=pltpu.SMEM)
    hbm = pl.BlockSpec(memory_space=pl.ANY)
    weight = pltpu.VMEM((slab, chunk), jnp.bfloat16)
    dma = pltpu.SemaphoreType.DMA
    return pl.pallas_call(
        functools.partial(kernel, n_param, n_proj),
        out_shape=jax.ShapeDtypeStruct((share, store_rows), jnp.float32),
        in_specs=[smem, smem, vmem, vmem, hbm, hbm],
        out_specs=vmem,
        scratch_shapes=[
            pltpu.VMEM((slabs, queries, slab), jnp.float32),
            pltpu.VMEM((store_rows, width), jnp.float32),
            pltpu.VMEM((2 * queries, coords), jnp.bfloat16),
            pltpu.VMEM((2 * cross_rows, width), jnp.bfloat16),
            pltpu.VMEM((coords // block, 32, width), jnp.bfloat16),
            weight, weight, weight, weight,
            pltpu.VMEM((queries, chunk), jnp.float32),
            pltpu.VMEM((queries, width), jnp.float32),
            pltpu.VMEM((chunks, queries // 2, chunk), jnp.float32),
            pltpu.VMEM((chunks, chips - 1, own, chunk), jnp.float32),
            pltpu.VMEM((queries, width), jnp.float32),
            pltpu.VMEM((queries, store_rows), jnp.float32),
            pltpu.VMEM((8, queries), jnp.float32),
            pltpu.VMEM((n_proj - 1, 8, queries), jnp.float32),
            pltpu.VMEM((queries, 128), jnp.float32),
            pltpu.VMEM((2, n_proj, tiles, share, tile), jnp.float32),
            pltpu.VMEM((3, 16, width), jnp.float32),
            pltpu.VMEM((queries, chunk), jnp.bfloat16),
            pltpu.VMEM((queries, chunk), jnp.bfloat16),
            dma((slabs,)),
            dma,
            dma((2, chunks)),
            dma((2, chunks, chips - 1)),
            dma((2, chunks, chips - 1)),
            dma((2, chunks)),
            dma((2, n_proj - 1)),
            dma((2, 2, n_proj, tiles)),
        ],
        compiler_params=pltpu.CompilerParams(
            collective_id=0, has_side_effects=True, vmem_limit_bytes=58 * 1024 * 1024
        ),
        name="attribution",
    )(offsets, proj_seed, bit_features(), pair_weights(), query_grads, stored)


def solution(mesh):
    placed = (P(None, "param"), P("param", "proj"), P(), P("param"))
    return jax.shard_map(
        on_device, mesh=mesh, in_specs=placed, out_specs=P("proj", "param"), check_vma=False
    )
```

```python
import functools
import math

import jax
import jax.numpy as jnp
import numpy as np
from jax import lax
from jax.experimental import pallas as pl
from jax.experimental.pallas import tpu as pltpu
from jax.sharding import PartitionSpec as P

modulus = 32749
middle = modulus // 2
epsilon = 1e-06
bits = 9
block = 1 << bits
pairs = [(p, q) for p in range(bits) for q in range(p + 1, bits)]
slab_blocks = 2
cross_rows = 48
to_whole = 1.5 * 2**23
slab = block * slab_blocks
chunk = 256
MESH = pl.DeviceIdType.MESH


def bit_features():
    digits = (np.arange(block)[:, None] >> np.arange(bits)[None, :]) & 1
    cross = np.stack([digits[:, p] * digits[:, q] for p, q in pairs], axis=1)
    vary = np.concatenate([digits, np.ones((block, 1), digits.dtype)], axis=1)
    out = np.zeros((block, 128), np.float32)
    for at in (0, cross_rows):
        out[:, at : at + len(pairs)] = cross
    for at in (2 * cross_rows, 2 * cross_rows + 16):
        out[:, at : at + bits + 1] = vary
    return jnp.asarray(out, jnp.bfloat16)


def pair_weights():
    out = np.zeros((cross_rows, 128), np.int32)
    for row, (p, q) in enumerate(pairs):
        out[row] = 2 ** (p + q + 1)
    return jnp.asarray(out)


def reduced(value):
    times = jnp.round(value.astype(jnp.float32) * (1.0 / modulus)).astype(jnp.int32)
    return value - times * modulus


def reduced_float(value):
    return value - ((value * (1.0 / modulus) + to_whole) - to_whole) * modulus


def two_pieces(value):
    high = ((value * (1.0 / 128) + to_whole) - to_whole) * 128.0
    return high.astype(jnp.bfloat16), (value - high).astype(jnp.bfloat16)


def split(value):
    high = value.astype(jnp.bfloat16)
    return high, (value - high.astype(jnp.float32)).astype(jnp.bfloat16)


def mix(a, b):
    return jnp.dot(a, b, preferred_element_type=jnp.float32)


def mix_rows(a, b):
    return lax.dot_general(a, b, (((1,), (1,)), ((), ())), preferred_element_type=jnp.float32)


def kernel(n_param, n_proj, offset_ref, seed_ref, feat_ref, weight_ref, grads_ref, stored_ref, out_ref,
           stage, store, both_q, cross, vary, high_a, low_a, high_b, low_b, total,
           part, pair_in, ring_in, proj, raw, square_out, square_in, column_sum, line_in, state, score_high, score_low,
           grad_sem, store_sem, pair_sem, ring_sem, gather_sem, back_sem, square_sem, line_sem):
    queries, coords = both_q.shape[0] // 2, both_q.shape[1]
    store_rows, width = store.shape
    slabs = coords // slab
    chunks = width // chunk
    chips = n_param // 2
    half = queries // 2
    own = half // chips
    share = queries // n_proj
    tile = min(store_rows, 256)
    tiles = store_rows // tile
    me = lax.axis_index("param")
    here = lax.axis_index("proj")
    core = lax.rem(me, 2)
    chip = lax.div(me, 2)
    sibling = me + 1 - 2 * core
    width_total = width * n_proj
    scale = 2.0 * math.sqrt(3.0 / (coords * n_param))

    def partner(o):
        return lax.rem(chip + o, chips)

    def fetch(s):
        return pltpu.make_async_copy(
            grads_ref.at[:, pl.ds(pl.multiple_of(s * slab, slab), slab)], stage.at[s], grad_sem.at[s]
        )

    for s in range(slabs):
        fetch(s).start()
    fetch_store = pltpu.make_async_copy(stored_ref, store, store_sem)
    fetch_store.start()

    barrier = pltpu.get_barrier_semaphore()
    pl.semaphore_signal(barrier, inc=1, device_id={"param": sibling}, device_id_type=MESH)
    for o in range(1, chips):
        pl.semaphore_signal(
            barrier, inc=1, device_id={"param": partner(o) * 2 + core}, device_id_type=MESH
        )
    for o in range(1, n_proj):
        pl.semaphore_signal(
            barrier, inc=1, device_id={"proj": lax.rem(here + o, n_proj)}, device_id_type=MESH
        )

    shape = (16, width)
    column = here * width + lax.broadcasted_iota(jnp.int32, shape, 1)
    row = lax.broadcasted_iota(jnp.int32, shape, 0)
    start = reduced(jnp.full(shape, offset_ref[0] * 1103 + seed_ref[0], jnp.int32))
    factor = reduced(column * 2111 + seed_ref[1]) + 1
    slope = reduced(factor * 1103)
    level = reduced((start + 3) * factor + 14)
    square = reduced(slope * slope)
    linear = reduced(reduced(slope * level) * 2 + 1103)
    constant = reduced(level * level + start)
    weights = jnp.concatenate([weight_ref[...]] * (width // 128), axis=1)
    pair_coef = reduced(jnp.concatenate([square] * (cross_rows // 16), axis=0) * weights)
    high, low = two_pieces(pair_coef.astype(jnp.float32))
    cross[pl.ds(0, cross_rows), :] = high
    cross[pl.ds(cross_rows, cross_rows), :] = low
    power = jnp.where(row < bits, jnp.left_shift(1, jnp.minimum(row, bits)), 0)
    first = reduced(reduced(square * power) * power + linear * power)
    first = jnp.where(row == bits, reduced(constant - middle), first)
    twice = reduced(square * (2 * block))
    step = reduced(twice * power)
    leap = reduced(reduced(square * block) * block + linear * block)
    step = jnp.where(row == bits, leap, step)
    bend = jnp.where(row == bits, reduced(twice * block), 0)
    state[0] = first.astype(jnp.float32)
    state[1] = step.astype(jnp.float32)
    state[2] = bend.astype(jnp.float32)

    @pl.loop(0, coords // block)
    def _(i):
        value = state[0]
        step = state[1]
        high, low = two_pieces(value)
        vary[i, pl.ds(0, 16), :] = high
        vary[i, pl.ds(16, 16), :] = low
        state[0] = reduced_float(value + step)
        state[1] = reduced_float(step + state[2])

    def prepare(s):
        fetch(s).wait()
        at = pl.ds(pl.multiple_of(s * slab, slab), slab)
        high, low = split(stage[s])
        both_q[pl.ds(0, queries), at] = high
        both_q[pl.ds(queries, queries), at] = low

    def make(t, high, low):
        s = lax.rem(t, slabs)
        at = pl.ds(pl.multiple_of(lax.div(t, slabs) * chunk, chunk), chunk)
        for b in range(slab_blocks):
            coef = jnp.concatenate([cross[:, at], vary[s * slab_blocks + b, :, at]], axis=0)
            x = mix(feat_ref[...], coef) * (1.0 / modulus)
            top, rest = split(x - ((x + to_whole) - to_whole))
            high[pl.ds(b * block, block), :] = top
            low[pl.ds(b * block, block), :] = rest

    def use(t, high, low):
        s = lax.rem(t, slabs)
        at = pl.ds(pl.multiple_of(s * slab, slab), slab)
        main = mix(both_q[:, at], high[...])
        rest = mix(both_q[pl.ds(0, queries), at], low[...])
        total[...] += main[:queries] + (main[queries:] + rest)

    def cols(n):
        return pl.ds(pl.multiple_of(n * chunk, chunk), chunk)

    def pair_copy(n):
        return pltpu.make_async_remote_copy(
            src_ref=part.at[pl.ds(pl.multiple_of((1 - core) * half, half), half), cols(n)],
            dst_ref=pair_in.at[n], send_sem=pair_sem.at[0, n], recv_sem=pair_sem.at[1, n],
            device_id={"param": sibling}, device_id_type=MESH,
        )

    def ring_copy(n, o):
        to = partner(o)
        return pltpu.make_async_remote_copy(
            src_ref=part.at[pl.ds(pl.multiple_of(core * half + to * own, own), own), cols(n)],
            dst_ref=ring_in.at[n, o - 1],
            send_sem=ring_sem.at[0, n, o - 1], recv_sem=ring_sem.at[1, n, o - 1],
            device_id={"param": to * 2 + core}, device_id_type=MESH,
        )

    own_rows = pl.ds(pl.multiple_of(core * half + chip * own, own), own)
    half_rows = pl.ds(pl.multiple_of(core * half, half), half)

    def gather_copy(n, o):
        return pltpu.make_async_remote_copy(
            src_ref=proj.at[own_rows, cols(n)], dst_ref=proj.at[own_rows, cols(n)],
            send_sem=gather_sem.at[0, n, o - 1], recv_sem=gather_sem.at[1, n, o - 1],
            device_id={"param": partner(o) * 2 + core}, device_id_type=MESH,
        )

    def back_copy(n):
        return pltpu.make_async_remote_copy(
            src_ref=proj.at[half_rows, cols(n)], dst_ref=proj.at[half_rows, cols(n)],
            send_sem=back_sem.at[0, n], recv_sem=back_sem.at[1, n],
            device_id={"param": sibling}, device_id_type=MESH,
        )

    def begin(n):
        column = here * width + n * chunk + lax.broadcasted_iota(jnp.int32, (1, chunk), 1)
        gain = jnp.sqrt(1.0 + column.astype(jnp.float32) * (2.0 / width_total)) * scale
        part[:, cols(n)] = total[...] * gain
        total[...] = jnp.zeros_like(total)
        pair_copy(n).start()

    def spread(n):
        pair_copy(n).wait_recv()
        part[half_rows, cols(n)] += pair_in[n]
        for o in range(1, chips):
            ring_copy(n, o).start()

    def join(n):
        value = part[own_rows, cols(n)]
        for o in range(1, chips):
            ring_copy(n, o).wait_recv()
            value += ring_in[n, o - 1]
        proj[own_rows, cols(n)] = value
        for o in range(1, chips):
            gather_copy(n, o).start()

    def hand_back(n):
        for o in range(1, chips):
            gather_copy(n, o).wait_recv()
        back_copy(n).start()

    def sums(n):
        back_copy(n).wait_recv()
        value = proj[:, cols(n)]
        high, low = split(value)
        score_high[...] = high
        score_low[...] = low
        squares = jnp.sum(value * value, axis=1, keepdims=True)
        column_sum[...] += jnp.broadcast_to(squares, (queries, 128))

    def score(n, r):
        at = pl.ds(pl.multiple_of(r * tile, tile), tile)
        sh, sl = split(store[at, cols(n)])
        high = score_high[...]
        raw[:, at] += mix_rows(high, sh) + mix_rows(score_low[...], sh) + mix_rows(high, sl)

    def scores(n):
        sums(n)

        @pl.loop(0, tiles)
        def _(r):
            score(n, r)

    def square_copy(o):
        return pltpu.make_async_remote_copy(
            src_ref=square_out, dst_ref=square_in.at[o - 1],
            send_sem=square_sem.at[0, o - 1], recv_sem=square_sem.at[1, o - 1],
            device_id={"proj": lax.rem(here + o, n_proj)}, device_id_type=MESH,
        )

    def piece(goal, p):
        return (
            pl.ds(pl.multiple_of(goal * share, share), share),
            pl.ds(pl.multiple_of(p * tile, tile), tile),
        )

    def line_copy(way, goal, p):
        return pltpu.make_async_remote_copy(
            src_ref=raw.at[piece(goal, p)], dst_ref=line_in.at[way, goal, p],
            send_sem=line_sem.at[0, way, goal, p], recv_sem=line_sem.at[1, way, goal, p],
            device_id={"proj": lax.rem(here + 1 - 2 * way + n_proj, n_proj)}, device_id_type=MESH,
        )

    def arrived(way, goal, p):
        line_copy(way, goal, p).wait_recv()
        raw[piece(goal, p)] += line_in[way, goal, p]

    late = (here >= (n_proj + 1) // 2).astype(jnp.int32)

    def moves(k, way):
        goal = (1 - way) * (n_proj - 1 - k) + way * k
        ahead = (goal - here) * (1 - 2 * way)
        behind = (1 - way) * here + way * (n_proj - 1 - here)
        return goal, ahead, behind

    total[...] = jnp.zeros_like(total)
    raw[...] = jnp.zeros_like(raw)
    column_sum[...] = jnp.zeros_like(column_sum)
    make(0, high_a, low_a)
    pl.semaphore_wait(barrier, n_param // 2 + n_proj - 1)
    turns = slabs // 2

    @pl.loop(0, chunks * turns)
    def _(it):
        t = it * 2

        @pl.when(it < turns)
        def _():
            prepare(t)
            prepare(t + 1)

        make(t + 1, high_b, low_b)
        use(t, high_a, low_a)
        make(jnp.minimum(t + 2, chunks * slabs - 1), high_a, low_a)
        use(t + 1, high_b, low_b)

        def after(delay, stage_of):
            turn = it - delay - (turns - 1)

            @pl.when((turn >= 0) & (lax.rem(turn + turns, turns) == 0))
            def _():
                stage_of(lax.div(turn, turns))

        after(0, begin)
        after(1, spread)
        after(3, join)
        after(5, hand_back)

        @pl.when(it == turns + 1)
        def _():
            fetch_store.wait()

        after(7, scores)

    last = chunks - 1
    spread(last)
    hand_back(last - 1)
    scores(last - 1)
    join(last)
    hand_back(last)
    sums(last)

    square_out[...] = column_sum[...].T[:8, :]
    for o in range(1, n_proj):
        square_copy(o).start()

    @pl.loop(0, tiles)
    def _(p):
        score(last, p)

        @pl.loop(0, n_proj - 1)
        def _(k):
            for way in range(2):
                goal, ahead, behind = moves(k, way)

                @pl.when((behind == 0) & (ahead > 0))
                def _():
                    line_copy(way, goal, p).start()

    def forward(way, p):
        @pl.loop(0, n_proj - 1)
        def _(k):
            goal, ahead, behind = moves(k, way)

            @pl.when((ahead > 0) & (behind > 0))
            def _():
                arrived(way, goal, p)
                line_copy(way, goal, p).start()

    @pl.loop(0, tiles + 1)
    def _(p):
        @pl.when(p < tiles)
        def _():
            forward(late, p)

        @pl.when(p > 0)
        def _():
            forward(1 - late, p - 1)

    whole = column_sum[...].T[:8, :]
    for o in range(1, n_proj):
        square_copy(o).wait_recv()
        whole += square_in[o - 1]
    inverse = lax.rsqrt(whole * (1.0 / width_total) + epsilon) * (1.0 / math.sqrt(width_total))
    column_sum[...] = jnp.broadcast_to(inverse[:1, :], (128, queries)).T

    @pl.loop(0, tiles)
    def _(p):
        @pl.when(here > 0)
        def _():
            arrived(0, here, p)

        @pl.when(here < n_proj - 1)
        def _():
            arrived(1, here, p)

        rows, at = piece(here, p)
        out_ref[:, at] = jnp.tanh(raw[rows, at] * column_sum[rows, :][:, :1])

    @pl.loop(0, chunks)
    def _(n):
        pair_copy(n).wait_send()
        back_copy(n).wait_send()
        for o in range(1, chips):
            ring_copy(n, o).wait_send()
            gather_copy(n, o).wait_send()

    for o in range(1, n_proj):
        square_copy(o).wait_send()

    @pl.loop(0, tiles)
    def _(p):
        @pl.loop(0, n_proj - 1)
        def _(k):
            for way in range(2):
                goal, ahead, behind = moves(k, way)

                @pl.when(ahead > 0)
                def _():
                    line_copy(way, goal, p).wait_send()


def on_device(query_grads, stored, proj_seed, offsets):
    n_param = lax.axis_size("param")
    n_proj = lax.axis_size("proj")
    queries, coords = query_grads.shape
    store_rows, width = stored.shape
    chips = n_param // 2
    chunks = width // chunk
    slabs = coords // slab
    share = queries // n_proj
    own = queries // n_param
    tile = min(store_rows, 256)
    tiles = store_rows // tile
    vmem = pl.BlockSpec(memory_space=pltpu.VMEM)
    smem = pl.BlockSpec(memory_space=pltpu.SMEM)
    hbm = pl.BlockSpec(memory_space=pl.ANY)
    weight = pltpu.VMEM((slab, chunk), jnp.bfloat16)
    dma = pltpu.SemaphoreType.DMA
    return pl.pallas_call(
        functools.partial(kernel, n_param, n_proj),
        out_shape=jax.ShapeDtypeStruct((share, store_rows), jnp.float32),
        in_specs=[smem, smem, vmem, vmem, hbm, hbm],
        out_specs=vmem,
        scratch_shapes=[
            pltpu.VMEM((slabs, queries, slab), jnp.float32),
            pltpu.VMEM((store_rows, width), jnp.float32),
            pltpu.VMEM((2 * queries, coords), jnp.bfloat16),
            pltpu.VMEM((2 * cross_rows, width), jnp.bfloat16),
            pltpu.VMEM((coords // block, 32, width), jnp.bfloat16),
            weight, weight, weight, weight,
            pltpu.VMEM((queries, chunk), jnp.float32),
            pltpu.VMEM((queries, width), jnp.float32),
            pltpu.VMEM((chunks, queries // 2, chunk), jnp.float32),
            pltpu.VMEM((chunks, chips - 1, own, chunk), jnp.float32),
            pltpu.VMEM((queries, width), jnp.float32),
            pltpu.VMEM((queries, store_rows), jnp.float32),
            pltpu.VMEM((8, queries), jnp.float32),
            pltpu.VMEM((n_proj - 1, 8, queries), jnp.float32),
            pltpu.VMEM((queries, 128), jnp.float32),
            pltpu.VMEM((2, n_proj, tiles, share, tile), jnp.float32),
            pltpu.VMEM((3, 16, width), jnp.float32),
            pltpu.VMEM((queries, chunk), jnp.bfloat16),
            pltpu.VMEM((queries, chunk), jnp.bfloat16),
            dma((slabs,)),
            dma,
            dma((2, chunks)),
            dma((2, chunks, chips - 1)),
            dma((2, chunks, chips - 1)),
            dma((2, chunks)),
            dma((2, n_proj - 1)),
            dma((2, 2, n_proj, tiles)),
        ],
        compiler_params=pltpu.CompilerParams(
            collective_id=0, has_side_effects=True, vmem_limit_bytes=58 * 1024 * 1024
        ),
        name="attribution",
    )(offsets, proj_seed, bit_features(), pair_weights(), query_grads, stored)


def solution(mesh):
    placed = (P(None, "param"), P("param", "proj"), P(), P("param"))
    return jax.shard_map(
        on_device, mesh=mesh, in_specs=placed, out_specs=P("proj", "param"), check_vma=False
    )
```

```python
import functools
import math

import jax
import jax.numpy as jnp
import numpy as np
from jax import lax
from jax.experimental import pallas as pl
from jax.experimental.pallas import tpu as pltpu
from jax.sharding import PartitionSpec as P

modulus = 32749
middle = modulus // 2
epsilon = 1e-06
bits = 9
block = 1 << bits
pairs = [(p, q) for p in range(bits) for q in range(p + 1, bits)]
slab_blocks = 2
cross_rows = 48
slab = block * slab_blocks
chunk = 256
MESH = pl.DeviceIdType.MESH


def bit_features():
    digits = (np.arange(block)[:, None] >> np.arange(bits)[None, :]) & 1
    cross = np.stack([digits[:, p] * digits[:, q] for p, q in pairs], axis=1)
    vary = np.concatenate([digits, np.ones((block, 1), digits.dtype)], axis=1)
    out = np.zeros((block, 128), np.float32)
    for at in (0, cross_rows):
        out[:, at : at + len(pairs)] = cross
    for at in (2 * cross_rows, 2 * cross_rows + 16):
        out[:, at : at + bits + 1] = vary
    return jnp.asarray(out, jnp.bfloat16)


def pair_weights():
    out = np.zeros((cross_rows, 128), np.int32)
    for row, (p, q) in enumerate(pairs):
        out[row] = 2 ** (p + q + 1)
    return jnp.asarray(out)


def reduced(value):
    times = jnp.round(value.astype(jnp.float32) * (1.0 / modulus)).astype(jnp.int32)
    return value - times * modulus


def reduced_float(value):
    return value - jnp.round(value * (1.0 / modulus)) * modulus


def two_pieces(value):
    high = jnp.round(value * (1.0 / 128)) * 128.0
    return high.astype(jnp.bfloat16), (value - high).astype(jnp.bfloat16)


def split(value):
    high = value.astype(jnp.bfloat16)
    return high, (value - high.astype(jnp.float32)).astype(jnp.bfloat16)


def mix(a, b):
    return jnp.dot(a, b, preferred_element_type=jnp.float32)


def mix_rows(a, b):
    return lax.dot_general(a, b, (((1,), (1,)), ((), ())), preferred_element_type=jnp.float32)


def kernel(n_param, n_proj, offset_ref, seed_ref, feat_ref, weight_ref, grads_ref, stored_ref, out_ref,
           stage, store, both_q, cross, vary, high_a, low_a, high_b, low_b, total,
           part, pair_in, ring_in, proj, raw, square_out, square_in, column_sum, line_in, state, score_high, score_low,
           grad_sem, store_sem, pair_sem, ring_sem, gather_sem, back_sem, square_sem, line_sem):
    queries, coords = both_q.shape[0] // 2, both_q.shape[1]
    store_rows, width = store.shape
    slabs = coords // slab
    chunks = width // chunk
    chips = n_param // 2
    half = queries // 2
    own = half // chips
    share = queries // n_proj
    tile = min(store_rows, 256)
    tiles = store_rows // tile
    strip = min(store_rows, 128)
    strips = store_rows // strip
    me = lax.axis_index("param")
    here = lax.axis_index("proj")
    core = lax.rem(me, 2)
    chip = lax.div(me, 2)
    sibling = me + 1 - 2 * core
    width_total = width * n_proj
    scale = 2.0 * math.sqrt(3.0 / (coords * n_param))

    def partner(o):
        return lax.rem(chip + o, chips)

    def fetch(s):
        return pltpu.make_async_copy(
            grads_ref.at[:, pl.ds(pl.multiple_of(s * slab, slab), slab)], stage.at[s], grad_sem.at[s]
        )

    for s in range(slabs):
        fetch(s).start()
    fetch_store = pltpu.make_async_copy(stored_ref, store, store_sem)
    fetch_store.start()

    barrier = pltpu.get_barrier_semaphore()
    pl.semaphore_signal(barrier, inc=1, device_id={"param": sibling}, device_id_type=MESH)
    for o in range(1, chips):
        pl.semaphore_signal(
            barrier, inc=1, device_id={"param": partner(o) * 2 + core}, device_id_type=MESH
        )
    for o in range(1, n_proj):
        pl.semaphore_signal(
            barrier, inc=1, device_id={"proj": lax.rem(here + o, n_proj)}, device_id_type=MESH
        )

    shape = (16, width)
    column = here * width + lax.broadcasted_iota(jnp.int32, shape, 1)
    row = lax.broadcasted_iota(jnp.int32, shape, 0)
    start = reduced(jnp.full(shape, offset_ref[0] * 1103 + seed_ref[0], jnp.int32))
    factor = reduced(column * 2111 + seed_ref[1]) + 1
    slope = reduced(factor * 1103)
    level = reduced((start + 3) * factor + 14)
    square = reduced(slope * slope)
    linear = reduced(reduced(slope * level) * 2 + 1103)
    constant = reduced(level * level + start)
    weights = jnp.concatenate([weight_ref[...]] * (width // 128), axis=1)
    pair_coef = reduced(jnp.concatenate([square] * (cross_rows // 16), axis=0) * weights)
    high, low = two_pieces(pair_coef.astype(jnp.float32))
    cross[pl.ds(0, cross_rows), :] = high
    cross[pl.ds(cross_rows, cross_rows), :] = low
    power = jnp.where(row < bits, jnp.left_shift(1, jnp.minimum(row, bits)), 0)
    first = reduced(reduced(square * power) * power + linear * power)
    first = jnp.where(row == bits, reduced(constant - middle), first)
    twice = reduced(square * (2 * block))
    step = reduced(twice * power)
    leap = reduced(reduced(square * block) * block + linear * block)
    step = jnp.where(row == bits, leap, step)
    bend = jnp.where(row == bits, reduced(twice * block), 0)
    state[0] = first.astype(jnp.float32)
    state[1] = step.astype(jnp.float32)
    state[2] = bend.astype(jnp.float32)

    @pl.loop(0, coords // block)
    def _(i):
        value = state[0]
        step = state[1]
        high, low = two_pieces(value)
        vary[i, pl.ds(0, 16), :] = high
        vary[i, pl.ds(16, 16), :] = low
        state[0] = reduced_float(value + step)
        state[1] = reduced_float(step + state[2])

    def prepare(s):
        fetch(s).wait()
        at = pl.ds(pl.multiple_of(s * slab, slab), slab)
        high, low = split(stage[s])
        both_q[pl.ds(0, queries), at] = high
        both_q[pl.ds(queries, queries), at] = low

    def make(t, high, low):
        s = lax.rem(t, slabs)
        at = pl.ds(pl.multiple_of(lax.div(t, slabs) * chunk, chunk), chunk)
        for b in range(slab_blocks):
            coef = jnp.concatenate([cross[:, at], vary[s * slab_blocks + b, :, at]], axis=0)
            x = mix(feat_ref[...], coef) * (1.0 / modulus)
            top, rest = split(x - jnp.round(x))
            high[pl.ds(b * block, block), :] = top
            low[pl.ds(b * block, block), :] = rest

    def use(t, high, low):
        s = lax.rem(t, slabs)
        at = pl.ds(pl.multiple_of(s * slab, slab), slab)
        main = mix(both_q[:, at], high[...])
        rest = mix(both_q[pl.ds(0, queries), at], low[...])
        total[...] += main[:queries] + (main[queries:] + rest)

    def cols(n):
        return pl.ds(pl.multiple_of(n * chunk, chunk), chunk)

    def pair_copy(n):
        return pltpu.make_async_remote_copy(
            src_ref=part.at[pl.ds(pl.multiple_of((1 - core) * half, half), half), cols(n)],
            dst_ref=pair_in.at[n], send_sem=pair_sem.at[0, n], recv_sem=pair_sem.at[1, n],
            device_id={"param": sibling}, device_id_type=MESH,
        )

    def ring_copy(n, o):
        to = partner(o)
        return pltpu.make_async_remote_copy(
            src_ref=part.at[pl.ds(pl.multiple_of(core * half + to * own, own), own), cols(n)],
            dst_ref=ring_in.at[n, o - 1],
            send_sem=ring_sem.at[0, n, o - 1], recv_sem=ring_sem.at[1, n, o - 1],
            device_id={"param": to * 2 + core}, device_id_type=MESH,
        )

    own_rows = pl.ds(pl.multiple_of(core * half + chip * own, own), own)
    half_rows = pl.ds(pl.multiple_of(core * half, half), half)

    def gather_copy(n, o):
        return pltpu.make_async_remote_copy(
            src_ref=proj.at[own_rows, cols(n)], dst_ref=proj.at[own_rows, cols(n)],
            send_sem=gather_sem.at[0, n, o - 1], recv_sem=gather_sem.at[1, n, o - 1],
            device_id={"param": partner(o) * 2 + core}, device_id_type=MESH,
        )

    def back_copy(n):
        return pltpu.make_async_remote_copy(
            src_ref=proj.at[half_rows, cols(n)], dst_ref=proj.at[half_rows, cols(n)],
            send_sem=back_sem.at[0, n], recv_sem=back_sem.at[1, n],
            device_id={"param": sibling}, device_id_type=MESH,
        )

    def begin(n):
        column = here * width + n * chunk + lax.broadcasted_iota(jnp.int32, (1, chunk), 1)
        gain = jnp.sqrt(1.0 + column.astype(jnp.float32) * (2.0 / width_total)) * scale
        part[:, cols(n)] = total[...] * gain
        total[...] = jnp.zeros_like(total)
        pair_copy(n).start()

    def spread(n):
        pair_copy(n).wait_recv()
        part[half_rows, cols(n)] += pair_in[n]
        for o in range(1, chips):
            ring_copy(n, o).start()

    def join(n):
        value = part[own_rows, cols(n)]
        for o in range(1, chips):
            ring_copy(n, o).wait_recv()
            value += ring_in[n, o - 1]
        proj[own_rows, cols(n)] = value
        for o in range(1, chips):
            gather_copy(n, o).start()

    def hand_back(n):
        for o in range(1, chips):
            gather_copy(n, o).wait_recv()
        back_copy(n).start()

    def sums(n):
        back_copy(n).wait_recv()
        value = proj[:, cols(n)]
        high, low = split(value)
        score_high[...] = high
        score_low[...] = low
        squares = jnp.sum(value * value, axis=1, keepdims=True)
        column_sum[...] += jnp.broadcast_to(squares, (queries, 128))

    def score(n, r):
        at = pl.ds(pl.multiple_of(r * tile, tile), tile)
        sh, sl = split(store[at, cols(n)])
        high = score_high[...]
        raw[:, at] += mix_rows(high, sh) + mix_rows(score_low[...], sh) + mix_rows(high, sl)

    def scores(n):
        sums(n)

        @pl.loop(0, tiles)
        def _(r):
            score(n, r)

    def square_copy(o):
        return pltpu.make_async_remote_copy(
            src_ref=square_out, dst_ref=square_in.at[o - 1],
            send_sem=square_sem.at[0, o - 1], recv_sem=square_sem.at[1, o - 1],
            device_id={"proj": lax.rem(here + o, n_proj)}, device_id_type=MESH,
        )

    def piece(goal, p):
        return (
            pl.ds(pl.multiple_of(goal * share, share), share),
            pl.ds(pl.multiple_of(p * strip, strip), strip),
        )

    def line_copy(way, goal, p):
        return pltpu.make_async_remote_copy(
            src_ref=raw.at[piece(goal, p)], dst_ref=line_in.at[way, goal, p],
            send_sem=line_sem.at[0, way, goal, p], recv_sem=line_sem.at[1, way, goal, p],
            device_id={"proj": lax.rem(here + 1 - 2 * way + n_proj, n_proj)}, device_id_type=MESH,
        )

    def arrived(way, goal, p):
        line_copy(way, goal, p).wait_recv()
        raw[piece(goal, p)] += line_in[way, goal, p]

    late = (here >= (n_proj + 1) // 2).astype(jnp.int32)

    def moves(k, way):
        goal = (1 - way) * (n_proj - 1 - k) + way * k
        ahead = (goal - here) * (1 - 2 * way)
        behind = (1 - way) * here + way * (n_proj - 1 - here)
        return goal, ahead, behind

    total[...] = jnp.zeros_like(total)
    raw[...] = jnp.zeros_like(raw)
    column_sum[...] = jnp.zeros_like(column_sum)
    make(0, high_a, low_a)
    pl.semaphore_wait(barrier, n_param // 2 + n_proj - 1)
    turns = slabs // 2

    @pl.loop(0, chunks * turns)
    def _(it):
        t = it * 2

        @pl.when(it < turns)
        def _():
            prepare(t)
            prepare(t + 1)

        make(t + 1, high_b, low_b)
        use(t, high_a, low_a)
        make(jnp.minimum(t + 2, chunks * slabs - 1), high_a, low_a)
        use(t + 1, high_b, low_b)

        def after(delay, stage_of):
            turn = it - delay - (turns - 1)

            @pl.when((turn >= 0) & (lax.rem(turn + turns, turns) == 0))
            def _():
                stage_of(lax.div(turn, turns))

        after(0, begin)
        after(1, spread)
        after(3, join)
        after(5, hand_back)

        @pl.when(it == turns + 1)
        def _():
            fetch_store.wait()

        after(7, scores)

    last = chunks - 1
    spread(last)
    hand_back(last - 1)
    scores(last - 1)
    join(last)
    hand_back(last)
    sums(last)

    square_out[...] = column_sum[...].T[:8, :]
    for o in range(1, n_proj):
        square_copy(o).start()

    @pl.loop(0, tiles)
    def _(p):
        score(last, p)
        for sub in range(strips // tiles):

            @pl.loop(0, n_proj - 1)
            def _(k):
                for way in range(2):
                    goal, ahead, behind = moves(k, way)

                    @pl.when((behind == 0) & (ahead > 0))
                    def _():
                        line_copy(way, goal, p * (strips // tiles) + sub).start()

    def forward(way, p):
        @pl.loop(0, n_proj - 1)
        def _(k):
            goal, ahead, behind = moves(k, way)

            @pl.when((ahead > 0) & (behind > 0))
            def _():
                arrived(way, goal, p)
                line_copy(way, goal, p).start()

    @pl.loop(0, strips + 1)
    def _(p):
        @pl.when(p < strips)
        def _():
            forward(late, p)

        @pl.when(p > 0)
        def _():
            forward(1 - late, p - 1)

    whole = column_sum[...].T[:8, :]
    for o in range(1, n_proj):
        square_copy(o).wait_recv()
        whole += square_in[o - 1]
    inverse = lax.rsqrt(whole * (1.0 / width_total) + epsilon) * (1.0 / math.sqrt(width_total))
    column_sum[...] = jnp.broadcast_to(inverse[:1, :], (128, queries)).T

    @pl.loop(0, strips)
    def _(p):
        @pl.when(here > 0)
        def _():
            arrived(0, here, p)

        @pl.when(here < n_proj - 1)
        def _():
            arrived(1, here, p)

        rows, at = piece(here, p)
        out_ref[:, at] = jnp.tanh(raw[rows, at] * column_sum[rows, :][:, :1])

    @pl.loop(0, chunks)
    def _(n):
        pair_copy(n).wait_send()
        back_copy(n).wait_send()
        for o in range(1, chips):
            ring_copy(n, o).wait_send()
            gather_copy(n, o).wait_send()

    for o in range(1, n_proj):
        square_copy(o).wait_send()

    @pl.loop(0, strips)
    def _(p):
        @pl.loop(0, n_proj - 1)
        def _(k):
            for way in range(2):
                goal, ahead, behind = moves(k, way)

                @pl.when(ahead > 0)
                def _():
                    line_copy(way, goal, p).wait_send()


def on_device(query_grads, stored, proj_seed, offsets):
    n_param = lax.axis_size("param")
    n_proj = lax.axis_size("proj")
    queries, coords = query_grads.shape
    store_rows, width = stored.shape
    chips = n_param // 2
    chunks = width // chunk
    slabs = coords // slab
    share = queries // n_proj
    own = queries // n_param
    tile = min(store_rows, 256)
    tiles = store_rows // tile
    strip = min(store_rows, 128)
    strips = store_rows // strip
    vmem = pl.BlockSpec(memory_space=pltpu.VMEM)
    smem = pl.BlockSpec(memory_space=pltpu.SMEM)
    hbm = pl.BlockSpec(memory_space=pl.ANY)
    weight = pltpu.VMEM((slab, chunk), jnp.bfloat16)
    dma = pltpu.SemaphoreType.DMA
    return pl.pallas_call(
        functools.partial(kernel, n_param, n_proj),
        out_shape=jax.ShapeDtypeStruct((share, store_rows), jnp.float32),
        in_specs=[smem, smem, vmem, vmem, hbm, hbm],
        out_specs=vmem,
        scratch_shapes=[
            pltpu.VMEM((slabs, queries, slab), jnp.float32),
            pltpu.VMEM((store_rows, width), jnp.float32),
            pltpu.VMEM((2 * queries, coords), jnp.bfloat16),
            pltpu.VMEM((2 * cross_rows, width), jnp.bfloat16),
            pltpu.VMEM((coords // block, 32, width), jnp.bfloat16),
            weight, weight, weight, weight,
            pltpu.VMEM((queries, chunk), jnp.float32),
            pltpu.VMEM((queries, width), jnp.float32),
            pltpu.VMEM((chunks, queries // 2, chunk), jnp.float32),
            pltpu.VMEM((chunks, chips - 1, own, chunk), jnp.float32),
            pltpu.VMEM((queries, width), jnp.float32),
            pltpu.VMEM((queries, store_rows), jnp.float32),
            pltpu.VMEM((8, queries), jnp.float32),
            pltpu.VMEM((n_proj - 1, 8, queries), jnp.float32),
            pltpu.VMEM((queries, 128), jnp.float32),
            pltpu.VMEM((2, n_proj, strips, share, strip), jnp.float32),
            pltpu.VMEM((3, 16, width), jnp.float32),
            pltpu.VMEM((queries, chunk), jnp.bfloat16),
            pltpu.VMEM((queries, chunk), jnp.bfloat16),
            dma((slabs,)),
            dma,
            dma((2, chunks)),
            dma((2, chunks, chips - 1)),
            dma((2, chunks, chips - 1)),
            dma((2, chunks)),
            dma((2, n_proj - 1)),
            dma((2, 2, n_proj, strips)),
        ],
        compiler_params=pltpu.CompilerParams(
            collective_id=0, has_side_effects=True, vmem_limit_bytes=58 * 1024 * 1024
        ),
        name="attribution",
    )(offsets, proj_seed, bit_features(), pair_weights(), query_grads, stored)


def solution(mesh):
    placed = (P(None, "param"), P("param", "proj"), P(), P("param"))
    return jax.shard_map(
        on_device, mesh=mesh, in_specs=placed, out_specs=P("proj", "param"), check_vma=False
    )
```

```python
import functools
import math

import jax
import jax.numpy as jnp
import numpy as np
from jax import lax
from jax.experimental import pallas as pl
from jax.experimental.pallas import tpu as pltpu
from jax.sharding import PartitionSpec as P

modulus = 32749
middle = modulus // 2
epsilon = 1e-06
bits = 9
block = 1 << bits
pairs = [(p, q) for p in range(bits) for q in range(p + 1, bits)]
slab_blocks = 2
cross_rows = 48
slab = block * slab_blocks
chunk = 256
MESH = pl.DeviceIdType.MESH


def bit_features():
    digits = (np.arange(block)[:, None] >> np.arange(bits)[None, :]) & 1
    cross = np.stack([digits[:, p] * digits[:, q] for p, q in pairs], axis=1)
    vary = np.concatenate([digits, np.ones((block, 1), digits.dtype)], axis=1)
    out = np.zeros((block, 128), np.float32)
    for at in (0, cross_rows):
        out[:, at : at + len(pairs)] = cross
    for at in (2 * cross_rows, 2 * cross_rows + 16):
        out[:, at : at + bits + 1] = vary
    return jnp.asarray(out, jnp.bfloat16)


def pair_weights():
    out = np.zeros((cross_rows, 128), np.int32)
    for row, (p, q) in enumerate(pairs):
        out[row] = 2 ** (p + q + 1)
    return jnp.asarray(out)


def reduced(value):
    times = jnp.round(value.astype(jnp.float32) * (1.0 / modulus)).astype(jnp.int32)
    return value - times * modulus


def reduced_float(value):
    return value - jnp.round(value * (1.0 / modulus)) * modulus


def two_pieces(value):
    high = jnp.round(value * (1.0 / 128)) * 128.0
    return high.astype(jnp.bfloat16), (value - high).astype(jnp.bfloat16)


def split(value):
    high = value.astype(jnp.bfloat16)
    return high, (value - high.astype(jnp.float32)).astype(jnp.bfloat16)


def mix(a, b):
    return jnp.dot(a, b, preferred_element_type=jnp.float32)


def mix_rows(a, b):
    return lax.dot_general(a, b, (((1,), (1,)), ((), ())), preferred_element_type=jnp.float32)


def kernel(n_param, n_proj, offset_ref, seed_ref, feat_ref, weight_ref, grads_ref, stored_ref, out_ref,
           stage, store, both_q, cross, vary, high_a, low_a, high_b, low_b, total,
           part, pair_in, ring_in, proj, raw, square_out, square_in, column_sum, line_in, state, score_high, score_low,
           grad_sem, store_sem, pair_sem, ring_sem, gather_sem, back_sem, square_sem, line_sem):
    queries, coords = both_q.shape[0] // 2, both_q.shape[1]
    store_rows, width = store.shape
    slabs = coords // slab
    chunks = width // chunk
    chips = n_param // 2
    half = queries // 2
    own = half // chips
    share = queries // n_proj
    tile = min(store_rows, 256)
    tiles = store_rows // tile
    me = lax.axis_index("param")
    here = lax.axis_index("proj")
    core = lax.rem(me, 2)
    chip = lax.div(me, 2)
    sibling = me + 1 - 2 * core
    width_total = width * n_proj
    scale = 2.0 * math.sqrt(3.0 / (coords * n_param))

    def partner(o):
        return lax.rem(chip + o, chips)

    def fetch(s):
        return pltpu.make_async_copy(
            grads_ref.at[:, pl.ds(pl.multiple_of(s * slab, slab), slab)], stage.at[s], grad_sem.at[s]
        )

    for s in range(slabs):
        fetch(s).start()
    fetch_store = pltpu.make_async_copy(stored_ref, store, store_sem)
    fetch_store.start()

    barrier = pltpu.get_barrier_semaphore()
    pl.semaphore_signal(barrier, inc=1, device_id={"param": sibling}, device_id_type=MESH)
    for o in range(1, chips):
        pl.semaphore_signal(
            barrier, inc=1, device_id={"param": partner(o) * 2 + core}, device_id_type=MESH
        )
    for o in range(1, n_proj):
        pl.semaphore_signal(
            barrier, inc=1, device_id={"proj": lax.rem(here + o, n_proj)}, device_id_type=MESH
        )

    shape = (16, width)
    column = here * width + lax.broadcasted_iota(jnp.int32, shape, 1)
    row = lax.broadcasted_iota(jnp.int32, shape, 0)
    start = reduced(jnp.full(shape, offset_ref[0] * 1103 + seed_ref[0], jnp.int32))
    factor = reduced(column * 2111 + seed_ref[1]) + 1
    slope = reduced(factor * 1103)
    level = reduced((start + 3) * factor + 14)
    square = reduced(slope * slope)
    linear = reduced(reduced(slope * level) * 2 + 1103)
    constant = reduced(level * level + start)
    weights = jnp.concatenate([weight_ref[...]] * (width // 128), axis=1)
    pair_coef = reduced(jnp.concatenate([square] * (cross_rows // 16), axis=0) * weights)
    high, low = two_pieces(pair_coef.astype(jnp.float32))
    cross[pl.ds(0, cross_rows), :] = high
    cross[pl.ds(cross_rows, cross_rows), :] = low
    power = jnp.where(row < bits, jnp.left_shift(1, jnp.minimum(row, bits)), 0)
    first = reduced(reduced(square * power) * power + linear * power)
    first = jnp.where(row == bits, reduced(constant - middle), first)
    twice = reduced(square * (2 * block))
    step = reduced(twice * power)
    leap = reduced(reduced(square * block) * block + linear * block)
    step = jnp.where(row == bits, leap, step)
    bend = jnp.where(row == bits, reduced(twice * block), 0)
    state[0] = first.astype(jnp.float32)
    state[1] = step.astype(jnp.float32)
    state[2] = bend.astype(jnp.float32)

    @pl.loop(0, coords // block)
    def _(i):
        value = state[0]
        step = state[1]
        high, low = two_pieces(value)
        vary[i, pl.ds(0, 16), :] = high
        vary[i, pl.ds(16, 16), :] = low
        state[0] = reduced_float(value + step)
        state[1] = reduced_float(step + state[2])

    def prepare(s):
        fetch(s).wait()
        at = pl.ds(pl.multiple_of(s * slab, slab), slab)
        high, low = split(stage[s])
        both_q[pl.ds(0, queries), at] = high
        both_q[pl.ds(queries, queries), at] = low

    def make(t, high, low):
        s = lax.rem(t, slabs)
        at = pl.ds(pl.multiple_of(lax.div(t, slabs) * chunk, chunk), chunk)
        for b in range(slab_blocks):
            coef = jnp.concatenate([cross[:, at], vary[s * slab_blocks + b, :, at]], axis=0)
            x = mix(feat_ref[...], coef) * (1.0 / modulus)
            top, rest = split(x - jnp.round(x))
            high[pl.ds(b * block, block), :] = top
            low[pl.ds(b * block, block), :] = rest

    def use(t, high, low):
        s = lax.rem(t, slabs)
        at = pl.ds(pl.multiple_of(s * slab, slab), slab)
        main = mix(both_q[:, at], high[...])
        rest = mix(both_q[pl.ds(0, queries), at], low[...])
        total[...] += main[:queries] + (main[queries:] + rest)

    def cols(n):
        return pl.ds(pl.multiple_of(n * chunk, chunk), chunk)

    def pair_copy(n):
        return pltpu.make_async_remote_copy(
            src_ref=part.at[pl.ds(pl.multiple_of((1 - core) * half, half), half), cols(n)],
            dst_ref=pair_in.at[n], send_sem=pair_sem.at[0, n], recv_sem=pair_sem.at[1, n],
            device_id={"param": sibling}, device_id_type=MESH,
        )

    def ring_copy(n, o):
        to = partner(o)
        return pltpu.make_async_remote_copy(
            src_ref=part.at[pl.ds(pl.multiple_of(core * half + to * own, own), own), cols(n)],
            dst_ref=ring_in.at[n, o - 1],
            send_sem=ring_sem.at[0, n, o - 1], recv_sem=ring_sem.at[1, n, o - 1],
            device_id={"param": to * 2 + core}, device_id_type=MESH,
        )

    own_rows = pl.ds(pl.multiple_of(core * half + chip * own, own), own)
    half_rows = pl.ds(pl.multiple_of(core * half, half), half)

    def gather_copy(n, o):
        return pltpu.make_async_remote_copy(
            src_ref=proj.at[own_rows, cols(n)], dst_ref=proj.at[own_rows, cols(n)],
            send_sem=gather_sem.at[0, n, o - 1], recv_sem=gather_sem.at[1, n, o - 1],
            device_id={"param": partner(o) * 2 + core}, device_id_type=MESH,
        )

    def back_copy(n):
        return pltpu.make_async_remote_copy(
            src_ref=proj.at[half_rows, cols(n)], dst_ref=proj.at[half_rows, cols(n)],
            send_sem=back_sem.at[0, n], recv_sem=back_sem.at[1, n],
            device_id={"param": sibling}, device_id_type=MESH,
        )

    def begin(n):
        column = here * width + n * chunk + lax.broadcasted_iota(jnp.int32, (1, chunk), 1)
        gain = jnp.sqrt(1.0 + column.astype(jnp.float32) * (2.0 / width_total)) * scale
        part[:, cols(n)] = total[...] * gain
        total[...] = jnp.zeros_like(total)
        pair_copy(n).start()

    def spread(n):
        pair_copy(n).wait_recv()
        part[half_rows, cols(n)] += pair_in[n]
        for o in range(1, chips):
            ring_copy(n, o).start()

    def join(n):
        value = part[own_rows, cols(n)]
        for o in range(1, chips):
            ring_copy(n, o).wait_recv()
            value += ring_in[n, o - 1]
        proj[own_rows, cols(n)] = value
        for o in range(1, chips):
            gather_copy(n, o).start()

    def hand_back(n):
        for o in range(1, chips):
            gather_copy(n, o).wait_recv()
        back_copy(n).start()

    def sums(n):
        back_copy(n).wait_recv()
        value = proj[:, cols(n)]
        high, low = split(value)
        score_high[...] = high
        score_low[...] = low

    def squares_of(n):
        value = proj[:, cols(n)]
        squares = jnp.sum(value * value, axis=1, keepdims=True)
        column_sum[...] += jnp.broadcast_to(squares, (queries, 128))

    def score(n, r):
        at = pl.ds(pl.multiple_of(r * tile, tile), tile)
        sh, sl = split(store[at, cols(n)])
        high = score_high[...]
        raw[:, at] += mix_rows(high, sh) + mix_rows(score_low[...], sh) + mix_rows(high, sl)

    def scores(n):
        sums(n)
        squares_of(n)

        @pl.loop(0, tiles)
        def _(r):
            score(n, r)

    def square_copy(o):
        return pltpu.make_async_remote_copy(
            src_ref=square_out, dst_ref=square_in.at[o - 1],
            send_sem=square_sem.at[0, o - 1], recv_sem=square_sem.at[1, o - 1],
            device_id={"proj": lax.rem(here + o, n_proj)}, device_id_type=MESH,
        )

    def piece(goal, p):
        return (
            pl.ds(pl.multiple_of(goal * share, share), share),
            pl.ds(pl.multiple_of(p * tile, tile), tile),
        )

    def line_copy(way, goal, p):
        return pltpu.make_async_remote_copy(
            src_ref=raw.at[piece(goal, p)], dst_ref=line_in.at[way, goal, p],
            send_sem=line_sem.at[0, way, goal, p], recv_sem=line_sem.at[1, way, goal, p],
            device_id={"proj": lax.rem(here + 1 - 2 * way + n_proj, n_proj)}, device_id_type=MESH,
        )

    def arrived(way, goal, p):
        line_copy(way, goal, p).wait_recv()
        raw[piece(goal, p)] += line_in[way, goal, p]

    late = (here >= (n_proj + 1) // 2).astype(jnp.int32)

    def moves(k, way):
        goal = (1 - way) * (n_proj - 1 - k) + way * k
        ahead = (goal - here) * (1 - 2 * way)
        behind = (1 - way) * here + way * (n_proj - 1 - here)
        return goal, ahead, behind

    total[...] = jnp.zeros_like(total)
    raw[...] = jnp.zeros_like(raw)
    column_sum[...] = jnp.zeros_like(column_sum)
    make(0, high_a, low_a)
    pl.semaphore_wait(barrier, n_param // 2 + n_proj - 1)
    turns = slabs // 2

    @pl.loop(0, chunks * turns)
    def _(it):
        t = it * 2

        @pl.when(it < turns)
        def _():
            prepare(t)
            prepare(t + 1)

        make(t + 1, high_b, low_b)
        use(t, high_a, low_a)
        make(jnp.minimum(t + 2, chunks * slabs - 1), high_a, low_a)
        use(t + 1, high_b, low_b)

        def after(delay, stage_of):
            turn = it - delay - (turns - 1)

            @pl.when((turn >= 0) & (lax.rem(turn + turns, turns) == 0))
            def _():
                stage_of(lax.div(turn, turns))

        after(0, begin)
        after(1, spread)
        after(3, join)
        after(5, hand_back)

        @pl.when(it == turns + 1)
        def _():
            fetch_store.wait()

        after(7, scores)

    last = chunks - 1
    spread(last)
    hand_back(last - 1)
    scores(last - 1)
    join(last)
    hand_back(last)
    sums(last)

    @pl.loop(0, tiles)
    def _(p):
        score(last, p)

        @pl.loop(0, n_proj - 1)
        def _(k):
            for way in range(2):
                goal, ahead, behind = moves(k, way)

                @pl.when((behind == 0) & (ahead > 0))
                def _():
                    line_copy(way, goal, p).start()

        @pl.when(p == 0)
        def _():
            squares_of(last)
            square_out[...] = column_sum[...].T[:8, :]
            for o in range(1, n_proj):
                square_copy(o).start()

    def forward(way, p):
        @pl.loop(0, n_proj - 1)
        def _(k):
            goal, ahead, behind = moves(k, way)

            @pl.when((ahead > 0) & (behind > 0))
            def _():
                arrived(way, goal, p)
                line_copy(way, goal, p).start()

    @pl.loop(0, tiles + 1)
    def _(p):
        @pl.when(p < tiles)
        def _():
            forward(late, p)

        @pl.when(p > 0)
        def _():
            forward(1 - late, p - 1)

    whole = column_sum[...].T[:8, :]
    for o in range(1, n_proj):
        square_copy(o).wait_recv()
        whole += square_in[o - 1]
    inverse = lax.rsqrt(whole * (1.0 / width_total) + epsilon) * (1.0 / math.sqrt(width_total))
    column_sum[...] = jnp.broadcast_to(inverse[:1, :], (128, queries)).T

    @pl.loop(0, tiles)
    def _(p):
        @pl.when(here > 0)
        def _():
            arrived(0, here, p)

        @pl.when(here < n_proj - 1)
        def _():
            arrived(1, here, p)

        rows, at = piece(here, p)
        out_ref[:, at] = jnp.tanh(raw[rows, at] * column_sum[rows, :][:, :1])

    @pl.loop(0, chunks)
    def _(n):
        pair_copy(n).wait_send()
        back_copy(n).wait_send()
        for o in range(1, chips):
            ring_copy(n, o).wait_send()
            gather_copy(n, o).wait_send()

    for o in range(1, n_proj):
        square_copy(o).wait_send()

    @pl.loop(0, tiles)
    def _(p):
        @pl.loop(0, n_proj - 1)
        def _(k):
            for way in range(2):
                goal, ahead, behind = moves(k, way)

                @pl.when(ahead > 0)
                def _():
                    line_copy(way, goal, p).wait_send()


def on_device(query_grads, stored, proj_seed, offsets):
    n_param = lax.axis_size("param")
    n_proj = lax.axis_size("proj")
    queries, coords = query_grads.shape
    store_rows, width = stored.shape
    chips = n_param // 2
    chunks = width // chunk
    slabs = coords // slab
    share = queries // n_proj
    own = queries // n_param
    tile = min(store_rows, 256)
    tiles = store_rows // tile
    vmem = pl.BlockSpec(memory_space=pltpu.VMEM)
    smem = pl.BlockSpec(memory_space=pltpu.SMEM)
    hbm = pl.BlockSpec(memory_space=pl.ANY)
    weight = pltpu.VMEM((slab, chunk), jnp.bfloat16)
    dma = pltpu.SemaphoreType.DMA
    return pl.pallas_call(
        functools.partial(kernel, n_param, n_proj),
        out_shape=jax.ShapeDtypeStruct((share, store_rows), jnp.float32),
        in_specs=[smem, smem, vmem, vmem, hbm, hbm],
        out_specs=vmem,
        scratch_shapes=[
            pltpu.VMEM((slabs, queries, slab), jnp.float32),
            pltpu.VMEM((store_rows, width), jnp.float32),
            pltpu.VMEM((2 * queries, coords), jnp.bfloat16),
            pltpu.VMEM((2 * cross_rows, width), jnp.bfloat16),
            pltpu.VMEM((coords // block, 32, width), jnp.bfloat16),
            weight, weight, weight, weight,
            pltpu.VMEM((queries, chunk), jnp.float32),
            pltpu.VMEM((queries, width), jnp.float32),
            pltpu.VMEM((chunks, queries // 2, chunk), jnp.float32),
            pltpu.VMEM((chunks, chips - 1, own, chunk), jnp.float32),
            pltpu.VMEM((queries, width), jnp.float32),
            pltpu.VMEM((queries, store_rows), jnp.float32),
            pltpu.VMEM((8, queries), jnp.float32),
            pltpu.VMEM((n_proj - 1, 8, queries), jnp.float32),
            pltpu.VMEM((queries, 128), jnp.float32),
            pltpu.VMEM((2, n_proj, tiles, share, tile), jnp.float32),
            pltpu.VMEM((3, 16, width), jnp.float32),
            pltpu.VMEM((queries, chunk), jnp.bfloat16),
            pltpu.VMEM((queries, chunk), jnp.bfloat16),
            dma((slabs,)),
            dma,
            dma((2, chunks)),
            dma((2, chunks, chips - 1)),
            dma((2, chunks, chips - 1)),
            dma((2, chunks)),
            dma((2, n_proj - 1)),
            dma((2, 2, n_proj, tiles)),
        ],
        compiler_params=pltpu.CompilerParams(
            collective_id=0, has_side_effects=True, vmem_limit_bytes=58 * 1024 * 1024
        ),
        name="attribution",
    )(offsets, proj_seed, bit_features(), pair_weights(), query_grads, stored)


def solution(mesh):
    placed = (P(None, "param"), P("param", "proj"), P(), P("param"))
    return jax.shard_map(
        on_device, mesh=mesh, in_specs=placed, out_specs=P("proj", "param"), check_vma=False
    )
```
